128 devices in a mesh: lon: 16 (over z, y_hi, core), lat: 8 (over x, y_lo).
Axes of the slice: x: 4, y: 4 (y_hi: 2, y_lo: 2; y = y_hi * 2 + y_lo), z: 4, core: 2. Of those that a mesh axis runs over, the one named last changes fastest.
Arguments:
- offset_input: bfloat16 [196, 64, 8192], P(None, 'lat', 'lon'), may hold values from -6 to 6
- current: bfloat16 [64, 64, 8192], P(None, 'lat', 'lon'), may hold values from -6 to 6
- source: bfloat16 [64, 64, 8192], P(None, 'lat', 'lon'), may hold values from -6 to 6
- first_weight: bfloat16 [9, 64, 196], replicated, may hold values from -0.125 to 0.125
- second_weight: bfloat16 [9, 64, 64], replicated, may hold values from -0.25 to 0.25
- mask_weight: bfloat16 [9, 144, 64], replicated, may hold values from -0.25 to 0.25
- deform_weight: bfloat16 [9, 64, 64], replicated, may hold values from -0.25 to 0.25
- merge_weight: bfloat16 [9, 64, 128], replicated, may hold values from -0.1875 to 0.1875
- residual_weight: bfloat16 [2, 2, 9, 64, 64], replicated, may hold values from -0.25 to 0.25
- footprint: int32 [64, 64, 9, 2], P('lat', 'lon'), may hold values from 0 to 4095, as said below
- tile_scale: float32 [64, 64, 9, 2], P('lat', 'lon'), may hold values from 0.5 to 2
- hats: bfloat16 [64, 64, 9, 2, 128, 128], P('lat', 'lon'), may hold values from -0.375 to 0.375
Outputs:
- propagated: bfloat16 [64, 64, 8192], P(None, 'lat', 'lon')
The draws below stay inside these ranges and needn't reach their ends.
Inputs may be any that keep to these rules, and one draw needn't show every extreme that they name: `footprint`: each id is row * 64 + block of a source block. For the reader at row y and block j the row lies within 2 of y (clamped to the frame) and the block lies within r blocks of j around the longitude loop, where r = max(1, ceil(2 |2 y - 63| / 64)) is 2 at the first and last rows; both distances are reached in every draw.
All inputs are finite; a program needn't handle non-finite values.
Results may differ from the reference program's by a relative error of at most 0.015.
Values may be sent and summed in bfloat16 or wider, within the bound.
A program may use at most 128 MiB of HBM per device.

```python
import math
import jax
import jax.numpy as jnp
from jax import lax

C = 64
GROUPS = 16
CIN = 196
BLK = 128
FP = 2
RY = 2
LB = 2
RES = 2
HEIGHT = 64
WB = 64
WIDTH = 8192


def draw_footprint(key, part):
    key = jax.random.fold_in(key, 11)
    first_key, second_key = jax.random.split(key)
    shape = (HEIGHT, WB, 9, FP)
    rows = jnp.arange(HEIGHT, dtype=jnp.int32)[:, None, None, None]
    columns = jnp.arange(WB, dtype=jnp.int32)[None, :, None, None]
    kernel_taps = jnp.arange(9, dtype=jnp.int32)[None, None, :, None]
    entries = jnp.arange(FP, dtype=jnp.int32)[None, None, None, :]
    reach = jnp.maximum(1, (LB * jnp.abs(2 * rows + 1 - HEIGHT) + HEIGHT - 1) // HEIGHT)
    raw_col = jax.random.randint(first_key, shape, 0, 1 << 20)
    col_move = raw_col % (2 * reach + 1) - reach
    row_move = jax.random.randint(second_key, shape, -RY, RY + 1)
    leading = entries == 0
    low_tap = leading & (kernel_taps == 0)
    high_tap = leading & (kernel_taps == 8)
    centre_tap = leading & (kernel_taps == 4)
    col_move = jnp.where(low_tap, -reach, col_move)
    row_move = jnp.where(low_tap, -RY, row_move)
    col_move = jnp.where(high_tap, reach, col_move)
    row_move = jnp.where(high_tap, RY, row_move)
    col_move = jnp.where(centre_tap, 0, col_move)
    row_move = jnp.where(centre_tap, 0, row_move)
    src_row = jnp.clip(rows + row_move, 0, HEIGHT - 1)
    src_col = (columns + col_move) % WB
    return (src_row * WB + src_col).astype(jnp.int32)


def block_levels(rng, extent, pieces, smallest, largest):
    loudness = 1.0
    for axis_at, parts in pieces:
        heights = jax.random.uniform(jax.random.fold_in(jax.random.fold_in(rng, 6), axis_at), (parts,), jnp.float32, smallest / len(pieces), largest / len(pieces))
        loudness = loudness * jnp.repeat(jnp.exp(heights), extent[axis_at] // parts).reshape((-1,) + (1,) * (len(extent) - 1 - axis_at))
    return loudness


def scatter_about(stream_key, shape, deviation, limit, pieces=(), held_as=jnp.bfloat16):
    drawn = deviation * jax.random.normal(stream_key, shape, jnp.float32)
    if pieces:
        drawn = drawn * block_levels(stream_key, shape, pieces, -0.22, 0.18)
    return jnp.clip(drawn, -limit, limit).astype(held_as)


def setup_inputs(seed: int = 0) -> dict:
    arg_keys = jax.random.split(jax.random.key(seed), 13)
    offset_input = scatter_about(arg_keys[0], (CIN, HEIGHT, WIDTH), 1.0, 6.0, ((1, 8), (2, 16)))
    current = scatter_about(arg_keys[1], (C, HEIGHT, WIDTH), 1.0, 6.0, ((1, 8), (2, 16)))
    source = scatter_about(arg_keys[2], (C, HEIGHT, WIDTH), 1.0, 6.0, ((1, 8), (2, 16)))
    first_weight = scatter_about(arg_keys[3], (9, C, CIN), (9 * CIN) ** -0.5, 0.125)
    second_weight = scatter_about(arg_keys[4], (9, C, C), (9 * C) ** -0.5, 0.25)
    mask_weight = scatter_about(arg_keys[5], (9, 9 * GROUPS, C), (9 * C) ** -0.5, 0.25)
    deform_weight = scatter_about(arg_keys[6], (9, C, C), (9 * C) ** -0.5, 0.25)
    merge_weight = scatter_about(arg_keys[7], (9, C, 2 * C), (18 * C) ** -0.5, 0.1875)
    residual_weight = scatter_about(arg_keys[8], (RES, 2, 9, C, C), (9 * C) ** -0.5, 0.25)
    footprint = draw_footprint(jax.random.fold_in(arg_keys[12], 71), 0)
    tile_scale = jnp.clip(jnp.exp(math.log(2.0) - 1.3862944 * jax.random.uniform(arg_keys[10], (HEIGHT, WB, 9, FP), jnp.float32) ** block_levels(arg_keys[10], (HEIGHT, WB, 9, FP), ((0, 8), (1, 16)), -0.2, 0.2)), 0.5, 2.0)
    hats = scatter_about(arg_keys[11], (HEIGHT, WB, 9, FP, BLK, BLK), (BLK * FP) ** -0.5, 0.375, ((0, 8), (1, 16)))
    return dict(offset_input=offset_input, current=current, source=source, first_weight=first_weight, second_weight=second_weight, mask_weight=mask_weight, deform_weight=deform_weight, merge_weight=merge_weight, residual_weight=residual_weight, footprint=footprint, tile_scale=tile_scale, hats=hats)


def leaky_unit(values):
    return jnp.where(values > 0, values, 0.1 * values)


def conv_full(values, weight):
    height = values.shape[1]
    width = values.shape[2]
    padded = jnp.pad(values, ((0, 0), (0, 0), (1, 1)), mode="wrap")
    padded = jnp.pad(padded, ((0, 0), (1, 1), (0, 0)))
    accumulated = jnp.zeros((weight.shape[1], height, width), jnp.float32)
    for kernel_tap in range(9):
        row_shift = kernel_tap // 3
        col_shift = kernel_tap % 3
        window = padded[:, row_shift:row_shift + height, col_shift:col_shift + width].astype(jnp.float32)
        accumulated = accumulated + jnp.einsum("oc,chw->ohw", weight[kernel_tap].astype(jnp.float32), window)
    return accumulated


def reference(offset_input, current, source, first_weight, second_weight, mask_weight, deform_weight, merge_weight, residual_weight, footprint, tile_scale, hats):
    hidden_one = leaky_unit(conv_full(offset_input, first_weight)).astype(jnp.bfloat16)
    hidden_two = leaky_unit(conv_full(hidden_one, second_weight)).astype(jnp.bfloat16)
    modulation = jax.nn.sigmoid(conv_full(hidden_two, mask_weight))
    src_blocks = source.reshape(C, HEIGHT, WB, BLK).transpose(1, 2, 0, 3).reshape(HEIGHT * WB, C, BLK)
    deform_float = deform_weight.astype(jnp.float32)

    def one_row(inputs):
        row_ids, row_hats, row_scale, row_mask = inputs
        picked = src_blocks[row_ids].astype(jnp.float32)
        products = jnp.einsum("jkfcs,jkfsd->jkfcd", picked, row_hats.astype(jnp.float32))
        sampled = jnp.sum(products * row_scale[:, :, :, None, None], axis=2)
        sampled = sampled.transpose(1, 2, 0, 3).reshape(9, C, WB * BLK)
        modulated = (row_mask.reshape(9, GROUPS, 1, WB * BLK) * sampled.reshape(9, GROUPS, C // GROUPS, WB * BLK))
        modulated = modulated.reshape(9, C, WB * BLK).astype(jnp.bfloat16)
        return jnp.einsum("koc,kcw->ow", deform_float, modulated.astype(jnp.float32)).astype(jnp.bfloat16)

    aligned = lax.map(one_row, (footprint, hats, tile_scale, modulation.transpose(1, 0, 2))).transpose(1, 0, 2)
    trunk = leaky_unit(conv_full(jnp.concatenate([current, aligned], axis=0), merge_weight)).astype(jnp.bfloat16)
    for block_index in range(RES):
        inner = jax.nn.relu(conv_full(trunk, residual_weight[block_index, 0])).astype(jnp.bfloat16)
        trunk = (trunk.astype(jnp.float32) + conv_full(inner, residual_weight[block_index, 1])).astype(jnp.bfloat16)
    return (trunk.astype(jnp.float32) + aligned.astype(jnp.float32)).astype(jnp.bfloat16)
```

```python
import functools

import jax
import jax.numpy as jnp
from jax import lax
from jax.experimental import pallas as pl
from jax.experimental.pallas import tpu as pltpu
from jax.sharding import PartitionSpec as P

BF = jnp.bfloat16
F32 = jnp.float32
MESH = pl.DeviceIdType.MESH

BLK = 128
ROWS = 8
COLS = 512
WIDE = 640
CIN = 196
CPAD = 256
NB = COLS // BLK
WIN_ROWS = ROWS + 4
WIN_COLS = NB + 4
TAPS = 9
K2 = 18

LEFT, RIGHT, UP, DOWN, UL, UR, DL, DR = range(8)
OPP = (RIGHT, LEFT, DOWN, UP, DR, DL, UR, UL)
S_OFF, S_SRC, S_SRC_LO, S_SRC_HI, S_CURM, S_CUR, S_PART, S_H1, S_ALM, S_AL, S_T0, S_T1 = range(12)


def leaky(v):
    return jnp.where(v > 0, v, 0.1 * v)


def kernel(
    n_lon, n_lat,
    off_hbm, cur_hbm, src_hbm, w1_ref, w2_ref, wm_ref, wd_ref, wg_ref, wr_ref,
    idx_ref, scale_ref, hats_hbm, out_ref,
    raw_off, raw_src, raw_cur, stage, hats, win, sampled, modulated,
    v0, h1, h2, joined, t0, i0, t1, i1,
    w1, w2, wm, wd, wg, wr,
    pack_off, got_off, pack_cur, got_cur, pack_al, got_al,
    part_out, part_in, part_own,
    load_sem, hat_sem, send_sem, recv_sem,
):
    lon = lax.axis_index("lon")
    lat = lax.axis_index("lat")
    left = lax.rem(lon + n_lon - 1, n_lon)
    right = lax.rem(lon + 1, n_lon)
    has_up = lat > 0
    has_down = lat < n_lat - 1
    nb = {
        LEFT: (None, (left, lat)), RIGHT: (None, (right, lat)),
        UP: (has_up, (lon, lat - 1)), DOWN: (has_down, (lon, lat + 1)),
        UL: (has_up, (left, lat - 1)), UR: (has_up, (right, lat - 1)),
        DL: (has_down, (left, lat + 1)), DR: (has_down, (right, lat + 1)),
    }

    def guarded(cond, fn):
        if cond is None:
            fn()
        else:
            pl.when(cond)(fn)

    def copy(kind, direction, src, dst):
        return pltpu.make_async_remote_copy(
            src_ref=src, dst_ref=dst,
            send_sem=send_sem.at[kind, direction],
            recv_sem=recv_sem.at[kind, OPP[direction]],
            device_id=nb[direction][1], device_id_type=MESH,
        )

    def send(kind, direction, src, dst):
        guarded(nb[direction][0], lambda: copy(kind, direction, src, dst).start())

    def wait_send(kind, direction, src):
        def go():
            pltpu.make_async_remote_copy(
                src_ref=src, dst_ref=src, send_sem=send_sem.at[kind, direction],
                recv_sem=recv_sem.at[kind, direction],
                device_id=nb[direction][1], device_id_type=MESH,
            ).wait_send()
        guarded(nb[direction][0], go)

    def wait_recv(kind, direction, dst):
        def go():
            pltpu.make_async_remote_copy(
                src_ref=dst, dst_ref=dst, send_sem=send_sem.at[kind, direction],
                recv_sem=recv_sem.at[kind, direction],
                device_id=nb[direction][1], device_id_type=MESH,
            ).wait_recv()
        guarded(nb[direction][0], go)

    load_off = pltpu.make_async_copy(off_hbm, raw_off, load_sem.at[0])
    load_src = pltpu.make_async_copy(src_hbm, raw_src, load_sem.at[1])
    load_cur = pltpu.make_async_copy(cur_hbm, raw_cur, load_sem.at[2])
    load_off.start()
    load_src.start()
    load_cur.start()

    def hat_load(y):
        return pltpu.make_async_copy(hats_hbm.at[y], hats.at[y], hat_sem.at[y])

    for y in range(ROWS):
        hat_load(y).start()

    def zero_rows(buf, lo, hi):
        buf[lo:hi] = jnp.zeros((hi - lo,) + buf.shape[1:], buf.dtype)

    for buf, m in ((h1, 2), (joined, 1), (t0, 2), (t1, 2)):
        zero_rows(buf, 0, m)
        zero_rows(buf, ROWS + m, ROWS + 2 * m)
    zero_rows(v0, 0, 1)
    zero_rows(v0, ROWS + 1, ROWS + 2)
    part_in[...] = jnp.zeros(part_in.shape, BF)
    got_cur[...] = jnp.zeros(got_cur.shape, BF)
    got_al[...] = jnp.zeros(got_al.shape, BF)
    pack_off[...] = jnp.zeros(pack_off.shape, BF)
    for i in range(1, ROWS + 1):
        v0[i, 192:CPAD, :] = jnp.zeros((CPAD - 192, WIDE), BF)

    barrier = pltpu.get_barrier_semaphore()
    for d in range(8):
        guarded(nb[d][0], lambda d=d: pl.semaphore_signal(
            barrier, inc=1, device_id=nb[d][1], device_id_type=MESH))
    both = has_up & has_down
    pl.when(both)(lambda: pl.semaphore_wait(barrier, 8))
    pl.when(jnp.logical_not(both))(lambda: pl.semaphore_wait(barrier, 5))

    lane = lax.broadcasted_iota(jnp.int32, (1, BLK), 1)

    def pack_tiles(tiles, side):
        total = None
        for y, tile in enumerate(tiles):
            shift = 8 * y if side == 0 else 8 * y + 8
            moved = pltpu.roll(tile, shift, 1) if shift else tile
            here = (lane >= 8 * y) & (lane < 8 * y + 8)
            total = jnp.where(here, moved, 0.0 if total is None else total)
        return total

    def unpack(from_right, from_left, y):
        a = pltpu.roll(from_right, (128 - 8 * y) % 128, 1) if y else from_right
        b = pltpu.roll(from_left, 120 - 8 * y, 1)
        return jnp.where(lane < 8, a, jnp.where(lane >= 120, b, 0.0))

    load_off.wait()
    for j in range(NB):
        stage[j] = raw_off[:, j * BLK:(j + 1) * BLK].astype(F32)

    def staged(channels, y, j):
        return stage[j, pl.ds(y, channels, stride=ROWS), :]

    pack_off[0, 0:CIN, :] = pack_tiles(
        [staged(CIN, y, 0) for y in range(ROWS)], 0).astype(BF)
    pack_off[1, 0:CIN, :] = pack_tiles(
        [staged(CIN, y, NB - 1) for y in range(ROWS)], 1).astype(BF)
    send(S_OFF, LEFT, pack_off.at[0], got_off.at[0])
    send(S_OFF, RIGHT, pack_off.at[1], got_off.at[1])

    def v0_row(y, _):
        for j in range(NB):
            v0[y + 1, 0:CIN, j * BLK:(j + 1) * BLK] = staged(CIN, y, j).astype(BF)
        return 0

    lax.fori_loop(0, ROWS, v0_row, 0)

    load_src.wait()
    for j in range(NB):
        stage[j, 0:512, :] = raw_src[:, j * BLK:(j + 1) * BLK].astype(F32)

    def win_row(y, _):
        for k in range(4):
            for j in range(NB):
                win[y + 2, j + 2, k * 16:(k + 1) * 16, :] = stage[
                    j, pl.ds(k * ROWS + y, 16, stride=4 * ROWS), :].astype(BF)
        return 0

    lax.fori_loop(0, ROWS, win_row, 0)
    w_lat_up, w_lat_dn = win.at[2:4, 2:6], win.at[8:10, 2:6]
    send(S_SRC, UP, w_lat_up, win.at[10:12, 2:6])
    send(S_SRC, DOWN, w_lat_dn, win.at[0:2, 2:6])
    w_left, w_right = win.at[2:10, 2:4], win.at[2:10, 4:6]
    send(S_SRC, LEFT, w_left, win.at[2:10, 6:8])
    send(S_SRC, RIGHT, w_right, win.at[2:10, 0:2])

    load_cur.wait()
    for j in range(NB):
        stage[j, 512:1024, :] = raw_cur[:, j * BLK:(j + 1) * BLK].astype(F32)

    def cur_staged(y, j):
        return stage[j, pl.ds(512 + y, 64, stride=ROWS), :]

    def cur_row(y, _):
        for j in range(NB):
            joined[y + 1, 0:64, j * BLK:(j + 1) * BLK] = cur_staged(y, j).astype(BF)
        return 0

    lax.fori_loop(0, ROWS, cur_row, 0)
    pack_cur[0] = pack_tiles([cur_staged(y, 0) for y in range(ROWS)], 0).astype(BF)
    pack_cur[1] = pack_tiles([cur_staged(y, NB - 1) for y in range(ROWS)], 1).astype(BF)

    w1[...] = jnp.zeros(w1.shape, BF)
    for a in range(3):
        for b in range(3):
            w1[b * 64:(b + 1) * 64, a * CPAD:a * CPAD + CIN] = w1_ref[3 * a + b]
            wg[b * 64:(b + 1) * 64, a * 128:(a + 1) * 128] = wg_ref[3 * a + b]
    for b in range(3):
        w2[b * 64:(b + 1) * 64, :] = jnp.concatenate([w2_ref[3 * a + b] for a in range(3)], axis=1)
        for r in range(4):
            wr[r, b * 64:(b + 1) * 64, :] = jnp.concatenate(
                [wr_ref[r, 3 * a + b] for a in range(3)], axis=1)
    wm[...] = jnp.concatenate([wm_ref[t] for t in range(TAPS)], axis=1)
    row_id = lax.broadcasted_iota(jnp.int32, (64, 64), 0)
    col_id = lax.broadcasted_iota(jnp.int32, (64, 64), 1)
    perm = (row_id == (col_id % 16) * 4 + col_id // 16).astype(BF)
    wd[...] = jnp.concatenate(
        [jnp.dot(wd_ref[t], perm, preferred_element_type=F32).astype(BF) for t in range(TAPS)], axis=1)

    def spread(p):
        n = p.shape[1]
        return pltpu.roll(p[0:64], 1, 1) + p[64:128] + pltpu.roll(p[128:192], n - 1, 1)

    def conv_row(src, i, weight):
        x = src[pl.ds(i, 3)].reshape(3 * src.shape[1], WIDE)
        return spread(jnp.dot(weight, x, preferred_element_type=F32))

    wait_recv(S_OFF, RIGHT, got_off.at[0])
    wait_recv(S_OFF, LEFT, got_off.at[1])
    for y in range(ROWS):
        v0[y + 1, 0:CIN, COLS:WIDE] = unpack(
            got_off[0, 0:CIN, :].astype(F32), got_off[1, 0:CIN, :].astype(F32), y).astype(BF)
    part_out[0] = spread(jnp.dot(w1[:, 2 * CPAD:], v0[1], preferred_element_type=F32)).astype(BF)
    part_out[1] = spread(jnp.dot(w1[:, :CPAD], v0[ROWS], preferred_element_type=F32)).astype(BF)
    send(S_PART, UP, part_out.at[0], part_in.at[1])
    send(S_PART, DOWN, part_out.at[1], part_in.at[0])

    def h1_row(y, _):
        h1[y + 2] = leaky(conv_row(v0, y, w1[...])).astype(BF)
        return 0

    part_own[0] = conv_row(v0, 0, w1[...])
    part_own[1] = conv_row(v0, ROWS - 1, w1[...])
    lax.fori_loop(1, ROWS - 1, h1_row, 0)

    wait_recv(S_SRC, UP, win.at[0:2, 2:6])
    wait_recv(S_SRC, DOWN, win.at[10:12, 2:6])

    def relay(kind, rows):
        send(kind, LEFT, win.at[rows, 2:4], win.at[rows, 6:8])
        send(kind, RIGHT, win.at[rows, 4:6], win.at[rows, 0:2])

    pl.when(has_up)(lambda: relay(S_SRC_LO, slice(0, 2)))
    pl.when(has_down)(lambda: relay(S_SRC_HI, slice(10, 12)))

    wait_recv(S_PART, UP, part_in.at[0])
    wait_recv(S_PART, DOWN, part_in.at[1])
    h1[2] = leaky(part_own[0] + part_in[0].astype(F32)).astype(BF)
    h1[ROWS + 1] = leaky(part_own[1] + part_in[1].astype(F32)).astype(BF)

    def edges_out(kind, buf, count, m):
        send(kind, UP, buf.at[m:m + count], buf.at[ROWS + m:ROWS + m + count])
        send(kind, DOWN, buf.at[ROWS + m - count:ROWS + m], buf.at[m - count:m])

    def edges_in(kind, buf, count, m):
        wait_recv(kind, UP, buf.at[m - count:m])
        wait_recv(kind, DOWN, buf.at[ROWS + m:ROWS + m + count])

    def edges_sent(kind, buf, count, m):
        wait_send(kind, UP, buf.at[m:m + count])
        wait_send(kind, DOWN, buf.at[ROWS + m - count:ROWS + m])

    edges_out(S_H1, h1, 2, 2)

    for side, dirs in ((0, (LEFT, UL, DL)), (1, (RIGHT, UR, DR))):
        for d in dirs:
            send(S_CURM, d, pack_cur.at[side], got_cur.at[OPP[d]])
    send(S_CUR, UP, joined.at[1, 0:64, 0:COLS], joined.at[ROWS + 1, 0:64, 0:COLS])
    send(S_CUR, DOWN, joined.at[ROWS, 0:64, 0:COLS], joined.at[0, 0:64, 0:COLS])

    def in_frame(y):
        g = lat * ROWS + y
        return (g >= 0) & (g < n_lat * ROWS)

    def h2_row(y, _):
        v = leaky(conv_row(h1, y + 1, w2[...]))
        v = jnp.where(in_frame(y), v, 0.0)
        h2[y + 1, 0:64] = pltpu.roll(v, 1, 1).astype(BF)
        h2[y + 1, 64:128] = v.astype(BF)
        h2[y + 1, 128:192] = pltpu.roll(v, WIDE - 1, 1).astype(BF)
        return 0

    lax.fori_loop(1, ROWS - 1, h2_row, 0)

    wait_recv(S_SRC, RIGHT, win.at[2:10, 6:8])
    wait_recv(S_SRC, LEFT, win.at[2:10, 0:2])

    def relayed(kind, rows):
        wait_recv(kind, RIGHT, win.at[rows, 6:8])
        wait_recv(kind, LEFT, win.at[rows, 0:2])

    pl.when(has_up)(lambda: relayed(S_SRC_LO, slice(0, 2)))
    pl.when(has_down)(lambda: relayed(S_SRC_HI, slice(10, 12)))

    for y in range(ROWS):
        hat_load(y).wait()

    def sample_row(y, _):
        for j in range(NB):
            for t in range(TAPS):
                at = (y * NB + j) * K2 + 2 * t
                parts = []
                for f in range(2):
                    ix = idx_ref[at + f]
                    blk = win[lax.shift_right_logical(ix, 3), lax.bitwise_and(ix, 7)]
                    parts.append((blk.astype(F32) * scale_ref[at + f]).astype(BF))
                tile = hats[y, (j * K2 + 2 * t) * BLK:(j * K2 + 2 * t + 2) * BLK, :]
                sampled[y, t * 64:(t + 1) * 64, j * BLK:(j + 1) * BLK] = jnp.dot(
                    jnp.concatenate(parts, axis=1), tile, preferred_element_type=F32)
        return 0

    lax.fori_loop(0, ROWS, sample_row, 0)

    def aligned_row(y, _):
        x = h2[pl.ds(y, 3)].reshape(576, WIDE)[:, 0:COLS]
        logits = jnp.dot(wm[...], x, preferred_element_type=F32)
        mod = 1.0 / (1.0 + jnp.exp(-logits))
        for t in range(TAPS):
            m = mod[t * 16:(t + 1) * 16]
            for k in range(4):
                lo = t * 64 + k * 16
                modulated[lo:lo + 16, :] = (m * sampled[y, lo:lo + 16, :]).astype(BF)
        joined[y + 1, 64:128, 0:COLS] = jnp.dot(
            wd[...], modulated[...], preferred_element_type=F32).astype(BF)
        return 0

    lax.fori_loop(2, ROWS - 2, aligned_row, 0)

    def edge4(fn):
        return lambda i, c: fn(i + (i // 2) * (ROWS - 4), c)

    def ring4(fn):
        return lambda i, c: fn(i - 1 + (i // 2) * (ROWS - 2), c)

    edges_in(S_H1, h1, 2, 2)
    lax.fori_loop(0, 4, ring4(h2_row), 0)
    lax.fori_loop(0, 4, edge4(aligned_row), 0)

    send(S_AL, UP, joined.at[1, 64:128, 0:COLS], joined.at[ROWS + 1, 64:128, 0:COLS])
    send(S_AL, DOWN, joined.at[ROWS, 64:128, 0:COLS], joined.at[0, 64:128, 0:COLS])
    pack_al[0] = pack_tiles(
        [joined[y + 1, 64:128, 0:BLK].astype(F32) for y in range(ROWS)], 0).astype(BF)
    pack_al[1] = pack_tiles(
        [joined[y + 1, 64:128, COLS - BLK:COLS].astype(F32) for y in range(ROWS)], 1).astype(BF)
    for side, dirs in ((0, (LEFT, UL, DL)), (1, (RIGHT, UR, DR))):
        for d in dirs:
            send(S_ALM, d, pack_al.at[side], got_al.at[OPP[d]])

    def margins(kind, got, lo):
        for d in range(8):
            if d not in (UP, DOWN):
                wait_recv(kind, d, got.at[d])

        def put(i, from_right, from_left, y):
            joined[i, lo:lo + 64, COLS:WIDE] = unpack(
                got[from_right].astype(F32), got[from_left].astype(F32), y).astype(BF)

        for y in range(ROWS):
            put(y + 1, RIGHT, LEFT, y)
        put(0, UR, UL, ROWS - 1)
        put(ROWS + 1, DR, DL, 0)

    margins(S_CURM, got_cur, 0)
    margins(S_ALM, got_al, 64)

    def t0_row(y, _):
        t0[y + 2] = leaky(conv_row(joined, y, wg[...])).astype(BF)
        return 0

    def inner_row(dst, src, r):
        def go(y, _):
            v = jnp.maximum(conv_row(src, y + 1, wr[r]), 0.0)
            dst[y + 1] = jnp.where(in_frame(y), v, 0.0).astype(BF)
            return 0
        return go

    def t1_row(y, _):
        t1[y + 2] = (t0[y + 2].astype(F32) + conv_row(i0, y, wr[1])).astype(BF)
        return 0

    def final_row(y, _):
        trunk = (t1[y + 2].astype(F32) + conv_row(i1, y, wr[3])).astype(BF)
        trunk = trunk[:, 0:COLS].astype(F32)
        total = trunk + joined[y + 1, 64:128, 0:COLS].astype(F32)
        for j in range(NB):
            stage[j, pl.ds(y, 64, stride=ROWS), :] = total[:, j * BLK:(j + 1) * BLK]
        return 0

    lax.fori_loop(1, ROWS - 1, t0_row, 0)
    wait_recv(S_CUR, UP, joined.at[0, 0:64, 0:COLS])
    wait_recv(S_CUR, DOWN, joined.at[ROWS + 1, 0:64, 0:COLS])
    wait_recv(S_AL, UP, joined.at[0, 64:128, 0:COLS])
    wait_recv(S_AL, DOWN, joined.at[ROWS + 1, 64:128, 0:COLS])
    t0_row(0, 0)
    t0_row(ROWS - 1, 0)
    edges_out(S_T0, t0, 2, 2)
    inner0 = inner_row(i0, t0, 0)
    inner1 = inner_row(i1, t1, 2)
    lax.fori_loop(1, ROWS - 1, inner0, 0)
    lax.fori_loop(2, ROWS - 2, t1_row, 0)
    edges_in(S_T0, t0, 2, 2)
    lax.fori_loop(0, 4, ring4(inner0), 0)
    lax.fori_loop(0, 4, edge4(t1_row), 0)
    edges_out(S_T1, t1, 2, 2)
    lax.fori_loop(1, ROWS - 1, inner1, 0)
    lax.fori_loop(2, ROWS - 2, final_row, 0)
    edges_in(S_T1, t1, 2, 2)
    lax.fori_loop(0, 4, ring4(inner1), 0)
    lax.fori_loop(0, 4, edge4(final_row), 0)
    for j in range(NB):
        out_ref[:, j * BLK:(j + 1) * BLK] = stage[j, 0:512, :].astype(BF)

    wait_send(S_OFF, LEFT, pack_off.at[0])
    wait_send(S_OFF, RIGHT, pack_off.at[1])
    wait_send(S_SRC, UP, w_lat_up)
    wait_send(S_SRC, DOWN, w_lat_dn)
    wait_send(S_SRC, LEFT, w_left)
    wait_send(S_SRC, RIGHT, w_right)

    def relay_sent(kind, rows):
        wait_send(kind, LEFT, win.at[rows, 2:4])
        wait_send(kind, RIGHT, win.at[rows, 4:6])

    pl.when(has_up)(lambda: relay_sent(S_SRC_LO, slice(0, 2)))
    pl.when(has_down)(lambda: relay_sent(S_SRC_HI, slice(10, 12)))
    wait_send(S_PART, UP, part_out.at[0])
    wait_send(S_PART, DOWN, part_out.at[1])
    for side, dirs in ((0, (LEFT, UL, DL)), (1, (RIGHT, UR, DR))):
        for d in dirs:
            wait_send(S_CURM, d, pack_cur.at[side])
            wait_send(S_ALM, d, pack_al.at[side])
    wait_send(S_CUR, UP, joined.at[1, 0:64, 0:COLS])
    wait_send(S_CUR, DOWN, joined.at[ROWS, 0:64, 0:COLS])
    wait_send(S_AL, UP, joined.at[1, 64:128, 0:COLS])
    wait_send(S_AL, DOWN, joined.at[ROWS, 64:128, 0:COLS])
    edges_sent(S_H1, h1, 2, 2)
    edges_sent(S_T0, t0, 2, 2)
    edges_sent(S_T1, t1, 2, 2)


def shards(
    offset_input, current, source, first_weight, second_weight, mask_weight, deform_weight,
    merge_weight, residual_weight, footprint, tile_scale, hats,
):
    n_lon, n_lat = lax.axis_size("lon"), lax.axis_size("lat")
    total_blocks = NB * n_lon
    row = footprint // total_blocks - lax.axis_index("lat") * ROWS + 2
    col = (footprint % total_blocks - lax.axis_index("lon") * NB + 2) % total_blocks
    index = (row * WIN_COLS + col).reshape(-1)
    vmem = pl.BlockSpec(memory_space=pltpu.VMEM)
    smem = pl.BlockSpec(memory_space=pltpu.SMEM)
    hbm = pl.BlockSpec(memory_space=pl.ANY)
    V = pltpu.VMEM
    out = pl.pallas_call(
        functools.partial(kernel, n_lon, n_lat),
        out_shape=jax.ShapeDtypeStruct((64 * ROWS, COLS), BF),
        in_specs=[hbm, hbm, hbm] + [vmem] * 6 + [smem, smem, hbm],
        out_specs=vmem,
        scratch_shapes=[
            V((CIN * ROWS, COLS), BF), V((64 * ROWS, COLS), BF), V((64 * ROWS, COLS), BF),
            V((NB, CIN * ROWS, BLK), F32),
            V((ROWS, NB * K2 * BLK, BLK), BF),
            V((WIN_ROWS, WIN_COLS, 64, BLK), BF),
            V((ROWS, TAPS * 64, COLS), F32),
            V((TAPS * 64, COLS), BF),
            V((ROWS + 2, CPAD, WIDE), BF),
            V((ROWS + 4, 64, WIDE), BF),
            V((ROWS + 2, 192, WIDE), BF),
            V((ROWS + 2, 128, WIDE), BF),
            V((ROWS + 4, 64, WIDE), BF),
            V((ROWS + 2, 64, WIDE), BF),
            V((ROWS + 4, 64, WIDE), BF),
            V((ROWS + 2, 64, WIDE), BF),
            V((192, 3 * CPAD), BF), V((192, 192), BF), V((144, 576), BF), V((64, 576), BF),
            V((192, 384), BF), V((4, 192, 192), BF),
            V((2, 208, BLK), BF), V((2, 208, BLK), BF),
            V((2, 64, BLK), BF), V((8, 64, BLK), BF),
            V((2, 64, BLK), BF), V((8, 64, BLK), BF),
            V((2, 64, WIDE), BF), V((2, 64, WIDE), BF), V((2, 64, WIDE), F32),
            pltpu.SemaphoreType.DMA((3,)),
            pltpu.SemaphoreType.DMA((ROWS,)),
            pltpu.SemaphoreType.DMA((12, 8)),
            pltpu.SemaphoreType.DMA((12, 8)),
        ],
        compiler_params=pltpu.CompilerParams(
            collective_id=0, has_side_effects=True, vmem_limit_bytes=60 * 2**20),
    )(
        offset_input.reshape(CIN * ROWS, COLS),
        current.reshape(64 * ROWS, COLS),
        source.reshape(64 * ROWS, COLS),
        first_weight, second_weight, mask_weight, deform_weight, merge_weight,
        residual_weight.reshape(4, 9, 64, 64),
        index, tile_scale.reshape(-1),
        hats.reshape(ROWS, NB * K2 * BLK, BLK),
    )
    return out.reshape(64, ROWS, COLS)


def solution(mesh):
    in_specs = (
        P(None, "lat", "lon"),
        P(None, "lat", "lon"),
        P(None, "lat", "lon"),
        P(),
        P(),
        P(),
        P(),
        P(),
        P(),
        P("lat", "lon", None, None),
        P("lat", "lon", None, None),
        P("lat", "lon", None, None, None, None),
    )
    return jax.shard_map(
        shards, mesh=mesh, in_specs=in_specs, out_specs=P(None, "lat", "lon"), check_vma=False)
```

```python
import functools

import jax
import jax.numpy as jnp
from jax import lax
from jax.experimental import pallas as pl
from jax.experimental.pallas import tpu as pltpu
from jax.sharding import PartitionSpec as P

BF = jnp.bfloat16
F32 = jnp.float32
MESH = pl.DeviceIdType.MESH

BLK = 128
ROWS = 8
COLS = 512
WIDE = 640
CIN = 196
CPAD = 256
NB = COLS // BLK
WIN_ROWS = ROWS + 4
WIN_COLS = NB + 4
TAPS = 9
K2 = 18

LEFT, RIGHT, UP, DOWN, UL, UR, DL, DR = range(8)
OPP = (RIGHT, LEFT, DOWN, UP, DR, DL, UR, UL)
(S_OFF, S_SRC, S_SRC_LO, S_SRC_HI, S_CURM, S_CUR, S_PART, S_H1, S_H1_IN, S_ALM, S_AL,
 S_T0, S_T0_IN, S_T1, S_T1_IN) = range(15)


def leaky(v):
    return jnp.where(v > 0, v, 0.1 * v)


def kernel(
    n_lon, n_lat,
    off_hbm, cur_hbm, src_hbm, w1_hbm, w2_hbm, wm_hbm, wd_hbm, wg_hbm, wr_hbm,
    foot_ref, scale_ref, hats_hbm, out_ref,
    w1_ref, w2_ref, wm_ref, wd_ref, wg_ref, wr_ref,
    raw_off, raw_src, raw_cur, stage, stage2, hats, win, sampled, modulated,
    v0, h1, h2, joined, t0, i0, t1, i1,
    w1, w2, wm, wd, wg, wr,
    pack_off, got_off, pack_cur, got_cur, pack_al, got_al,
    part_out, part_in, part_own,
    load_sem, hat_sem, send_sem, recv_sem,
):
    lon = lax.axis_index("lon")
    lat = lax.axis_index("lat")
    left = lax.rem(lon + n_lon - 1, n_lon)
    right = lax.rem(lon + 1, n_lon)
    has_up = lat > 0
    has_down = lat < n_lat - 1
    nb = {
        LEFT: (None, (left, lat)), RIGHT: (None, (right, lat)),
        UP: (has_up, (lon, lat - 1)), DOWN: (has_down, (lon, lat + 1)),
        UL: (has_up, (left, lat - 1)), UR: (has_up, (right, lat - 1)),
        DL: (has_down, (left, lat + 1)), DR: (has_down, (right, lat + 1)),
    }

    def guarded(cond, fn):
        if cond is None:
            fn()
        else:
            pl.when(cond)(fn)

    def copy(kind, direction, src, dst):
        return pltpu.make_async_remote_copy(
            src_ref=src, dst_ref=dst,
            send_sem=send_sem.at[kind, direction],
            recv_sem=recv_sem.at[kind, OPP[direction]],
            device_id=nb[direction][1], device_id_type=MESH,
        )

    def send(kind, direction, src, dst):
        guarded(nb[direction][0], lambda: copy(kind, direction, src, dst).start())

    def wait_send(kind, direction, src):
        def go():
            pltpu.make_async_remote_copy(
                src_ref=src, dst_ref=src, send_sem=send_sem.at[kind, direction],
                recv_sem=recv_sem.at[kind, direction],
                device_id=nb[direction][1], device_id_type=MESH,
            ).wait_send()
        guarded(nb[direction][0], go)

    def wait_recv(kind, direction, dst):
        def go():
            pltpu.make_async_remote_copy(
                src_ref=dst, dst_ref=dst, send_sem=send_sem.at[kind, direction],
                recv_sem=recv_sem.at[kind, direction],
                device_id=nb[direction][1], device_id_type=MESH,
            ).wait_recv()
        guarded(nb[direction][0], go)

    load_off = pltpu.make_async_copy(off_hbm, raw_off, load_sem.at[0])
    load_src = pltpu.make_async_copy(src_hbm, raw_src, load_sem.at[1])
    load_cur = pltpu.make_async_copy(cur_hbm, raw_cur, load_sem.at[2])
    load_off.start()
    load_src.start()
    load_weights = [
        pltpu.make_async_copy(a, b, load_sem.at[3 + n])
        for n, (a, b) in enumerate((
            (w1_hbm, w1_ref), (w2_hbm, w2_ref), (wm_hbm, wm_ref), (wd_hbm, wd_ref),
            (wg_hbm, wg_ref), (wr_hbm, wr_ref)))
    ]
    for load in load_weights:
        load.start()
    load_cur.start()

    def hat_load(y):
        return pltpu.make_async_copy(hats_hbm.at[y], hats.at[y], hat_sem.at[y])

    for y in range(ROWS):
        hat_load(y).start()

    def zero_rows(buf, lo, hi):
        buf[lo:hi] = jnp.zeros((hi - lo,) + buf.shape[1:], buf.dtype)

    def no_halo(top):
        for buf, m in ((h1, 2), (joined, 1), (t0, 2), (t1, 2)):
            if top:
                zero_rows(buf, 0, m)
            else:
                zero_rows(buf, ROWS + m, ROWS + 2 * m)
        n = 0 if top else 1
        zero_rows(part_in, n, n + 1)
        for d in (UL, UR) if top else (DL, DR):
            zero_rows(got_cur, d, d + 1)
            zero_rows(got_al, d, d + 1)

    pl.when(jnp.logical_not(has_up))(lambda: no_halo(True))
    pl.when(jnp.logical_not(has_down))(lambda: no_halo(False))

    barrier = pltpu.get_barrier_semaphore()
    for d in range(8):
        guarded(nb[d][0], lambda d=d: pl.semaphore_signal(
            barrier, inc=1, device_id=nb[d][1], device_id_type=MESH))

    def all_here():
        both = has_up & has_down
        pl.when(both)(lambda: pl.semaphore_wait(barrier, 8))
        pl.when(jnp.logical_not(both))(lambda: pl.semaphore_wait(barrier, 5))

    zero_rows(v0, 0, 1)
    zero_rows(v0, ROWS + 1, ROWS + 2)
    pack_off[...] = jnp.zeros(pack_off.shape, BF)
    for i in range(1, ROWS + 1):
        v0[i, 192:CPAD, :] = jnp.zeros((CPAD - 192, WIDE), BF)

    lane = lax.broadcasted_iota(jnp.int32, (1, BLK), 1)

    def pack_tiles(tiles, side):
        total = None
        for y, tile in enumerate(tiles):
            shift = 8 * y if side == 0 else 8 * y + 8
            moved = pltpu.roll(tile, shift, 1) if shift else tile
            here = (lane >= 8 * y) & (lane < 8 * y + 8)
            total = jnp.where(here, moved, 0.0 if total is None else total)
        return total

    def unpack(from_right, from_left, y):
        a = pltpu.roll(from_right, (128 - 8 * y) % 128, 1) if y else from_right
        b = pltpu.roll(from_left, 120 - 8 * y, 1)
        return jnp.where(lane < 8, a, jnp.where(lane >= 120, b, 0.0))

    load_off.wait()
    def stage_off(j):
        stage[j] = raw_off[:, j * BLK:(j + 1) * BLK].astype(F32)

    stage_off(0)
    stage_off(NB - 1)

    def staged(channels, y, j):
        return stage[j, pl.ds(y, channels, stride=ROWS), :]

    pack_off[0, 0:CIN, :] = pack_tiles(
        [staged(CIN, y, 0) for y in range(ROWS)], 0).astype(BF)
    pack_off[1, 0:CIN, :] = pack_tiles(
        [staged(CIN, y, NB - 1) for y in range(ROWS)], 1).astype(BF)
    all_here()
    send(S_OFF, LEFT, pack_off.at[0], got_off.at[0])
    send(S_OFF, RIGHT, pack_off.at[1], got_off.at[1])

    load_src.wait()
    for j in range(NB):
        stage2[j] = raw_src[:, j * BLK:(j + 1) * BLK].astype(F32)

    def win_row(y, _):
        for k in range(4):
            for j in range(NB):
                win[y + 2, j + 2, k * 16:(k + 1) * 16, :] = stage2[
                    j, pl.ds(k * ROWS + y, 16, stride=4 * ROWS), :].astype(BF)
        return 0

    lax.fori_loop(0, ROWS, win_row, 0)
    w_lat_up, w_lat_dn = win.at[2:4, 2:6], win.at[8:10, 2:6]
    send(S_SRC, UP, w_lat_up, win.at[10:12, 2:6])
    send(S_SRC, DOWN, w_lat_dn, win.at[0:2, 2:6])
    w_left, w_right = win.at[2:10, 2:4], win.at[2:10, 4:6]
    send(S_SRC, LEFT, w_left, win.at[2:10, 6:8])
    send(S_SRC, RIGHT, w_right, win.at[2:10, 0:2])

    for j in range(1, NB - 1):
        stage_off(j)

    def v0_row(y, _):
        for j in range(NB):
            v0[y + 1, 0:CIN, j * BLK:(j + 1) * BLK] = staged(CIN, y, j).astype(BF)
        return 0

    lax.fori_loop(0, ROWS, v0_row, 0)

    load_cur.wait()
    for j in range(NB):
        stage2[j] = raw_cur[:, j * BLK:(j + 1) * BLK].astype(F32)

    def cur_staged(y, j):
        return stage2[j, pl.ds(y, 64, stride=ROWS), :]

    def cur_row(y, _):
        for j in range(NB):
            joined[y + 1, 0:64, j * BLK:(j + 1) * BLK] = cur_staged(y, j).astype(BF)
        return 0

    lax.fori_loop(0, ROWS, cur_row, 0)
    pack_cur[0] = pack_tiles([cur_staged(y, 0) for y in range(ROWS)], 0).astype(BF)
    pack_cur[1] = pack_tiles([cur_staged(y, NB - 1) for y in range(ROWS)], 1).astype(BF)

    for load in load_weights:
        load.wait()
    w1[...] = jnp.zeros(w1.shape, BF)
    for a in range(3):
        for b in range(3):
            w1[b * 64:(b + 1) * 64, a * CPAD:a * CPAD + CIN] = w1_ref[3 * a + b]
            wg[b * 64:(b + 1) * 64, a * 128:(a + 1) * 128] = wg_ref[3 * a + b]
    for b in range(3):
        w2[b * 64:(b + 1) * 64, :] = jnp.concatenate([w2_ref[3 * a + b] for a in range(3)], axis=1)
        for r in range(4):
            wr[r, b * 64:(b + 1) * 64, :] = jnp.concatenate(
                [wr_ref[r, 3 * a + b] for a in range(3)], axis=1)
    wm[...] = wm_ref[...].reshape(TAPS * 64, 144).astype(F32).T.astype(BF)
    row_id = lax.broadcasted_iota(jnp.int32, (64, 64), 0)
    col_id = lax.broadcasted_iota(jnp.int32, (64, 64), 1)
    perm = (row_id == (col_id % 16) * 4 + col_id // 16).astype(BF)
    wd[...] = jnp.concatenate(
        [jnp.dot(wd_ref[t], perm, preferred_element_type=F32).astype(BF) for t in range(TAPS)], axis=1)

    def spread(p):
        n = p.shape[1]
        return pltpu.roll(p[0:64], 1, 1) + p[64:128] + pltpu.roll(p[128:192], n - 1, 1)

    def conv_row(src, i, weight):
        x = src[pl.ds(i, 3)].reshape(3 * src.shape[1], WIDE)
        return spread(jnp.dot(weight, x, preferred_element_type=F32))

    def row_out(kind, buf, m, n):
        send(kind, UP, buf.at[m + n], buf.at[ROWS + m + n])
        send(kind, DOWN, buf.at[ROWS + m - 1 - n], buf.at[m - 1 - n])

    def row_in(kind, buf, m, n):
        wait_recv(kind, UP, buf.at[m - 1 - n])
        wait_recv(kind, DOWN, buf.at[ROWS + m + n])

    def row_sent(kind, buf, m, n):
        wait_send(kind, UP, buf.at[m + n])
        wait_send(kind, DOWN, buf.at[ROWS + m - 1 - n])

    def rows_loop(lo, hi, fn):
        lax.fori_loop(lo, hi, fn, 0, unroll=True)

    wait_recv(S_OFF, RIGHT, got_off.at[0])
    wait_recv(S_OFF, LEFT, got_off.at[1])
    for y in range(ROWS):
        v0[y + 1, 0:CIN, COLS:WIDE] = unpack(
            got_off[0, 0:CIN, :].astype(F32), got_off[1, 0:CIN, :].astype(F32), y).astype(BF)
    part_out[0] = spread(jnp.dot(w1[:, 2 * CPAD:], v0[1], preferred_element_type=F32)).astype(BF)
    part_out[1] = spread(jnp.dot(w1[:, :CPAD], v0[ROWS], preferred_element_type=F32)).astype(BF)
    send(S_PART, UP, part_out.at[0], part_in.at[1])
    send(S_PART, DOWN, part_out.at[1], part_in.at[0])

    def h1_row(y, _):
        h1[y + 2] = leaky(conv_row(v0, y, w1[...])).astype(BF)
        return 0

    h1_row(1, 0)
    h1_row(ROWS - 2, 0)
    row_out(S_H1_IN, h1, 2, 1)
    rows_loop(2, ROWS - 2, h1_row)
    part_own[0] = conv_row(v0, 0, w1[...])
    part_own[1] = conv_row(v0, ROWS - 1, w1[...])

    wait_recv(S_SRC, UP, win.at[0:2, 2:6])
    wait_recv(S_SRC, DOWN, win.at[10:12, 2:6])

    def relay(kind, rows):
        send(kind, LEFT, win.at[rows, 2:4], win.at[rows, 6:8])
        send(kind, RIGHT, win.at[rows, 4:6], win.at[rows, 0:2])

    pl.when(has_up)(lambda: relay(S_SRC_LO, slice(0, 2)))
    pl.when(has_down)(lambda: relay(S_SRC_HI, slice(10, 12)))

    wait_recv(S_PART, UP, part_in.at[0])
    wait_recv(S_PART, DOWN, part_in.at[1])
    h1[2] = leaky(part_own[0] + part_in[0].astype(F32)).astype(BF)
    h1[ROWS + 1] = leaky(part_own[1] + part_in[1].astype(F32)).astype(BF)

    row_out(S_H1, h1, 2, 0)

    for side, dirs in ((0, (LEFT, UL, DL)), (1, (RIGHT, UR, DR))):
        for d in dirs:
            send(S_CURM, d, pack_cur.at[side], got_cur.at[OPP[d]])
    send(S_CUR, UP, joined.at[1, 0:64, 0:COLS], joined.at[ROWS + 1, 0:64, 0:COLS])
    send(S_CUR, DOWN, joined.at[ROWS, 0:64, 0:COLS], joined.at[0, 0:64, 0:COLS])

    def in_frame(y):
        g = lat * ROWS + y
        return (g >= 0) & (g < n_lat * ROWS)

    def h2_row(y, _):
        v = leaky(conv_row(h1, y + 1, w2[...]))
        v = jnp.where(in_frame(y), v, 0.0)
        h2[y + 1, 0:64] = pltpu.roll(v, 1, 1).astype(BF)
        h2[y + 1, 64:128] = v.astype(BF)
        h2[y + 1, 128:192] = pltpu.roll(v, WIDE - 1, 1).astype(BF)
        return 0

    rows_loop(1, ROWS - 1, h2_row)

    wait_recv(S_SRC, RIGHT, win.at[2:10, 6:8])
    wait_recv(S_SRC, LEFT, win.at[2:10, 0:2])

    def relayed(kind, rows):
        wait_recv(kind, RIGHT, win.at[rows, 6:8])
        wait_recv(kind, LEFT, win.at[rows, 0:2])

    pl.when(has_up)(lambda: relayed(S_SRC_LO, slice(0, 2)))
    pl.when(has_down)(lambda: relayed(S_SRC_HI, slice(10, 12)))

    for y in range(ROWS):
        hat_load(y).wait()

    total = NB * n_lon
    shift = total.bit_length() - 1
    row_base = lat * ROWS - 2
    col_base = lon * NB - 2

    def sample_row(y, _):
        for j in range(NB):
            for t in range(TAPS):
                parts = []
                for f in range(2):
                    ix = foot_ref[y, j, f, t]
                    row = jnp.clip(lax.shift_right_logical(ix, shift) - row_base, 0, WIN_ROWS - 1)
                    col = jnp.minimum(lax.bitwise_and(ix - col_base, total - 1), WIN_COLS - 1)
                    parts.append((win[row, col].astype(F32) * scale_ref[y, j, f, t]).astype(BF))
                tile = hats[y, (j * K2 + 2 * t) * BLK:(j * K2 + 2 * t + 2) * BLK, :]
                sampled[y, t * 64:(t + 1) * 64, j * BLK:(j + 1) * BLK] = jnp.dot(
                    jnp.concatenate(parts, axis=1), tile, preferred_element_type=F32)
        return 0

    lax.fori_loop(0, ROWS, sample_row, 0, unroll=2)

    def aligned_row(y, _):
        x = h2[pl.ds(y, 3)].reshape(576, WIDE)[:, 0:COLS]
        logits = jnp.dot(wm[...], x, preferred_element_type=F32)
        mod = 1.0 / (1.0 + jnp.exp(-logits))
        for t in range(TAPS):
            m = mod[t * 16:(t + 1) * 16]
            for k in range(4):
                lo = t * 64 + k * 16
                modulated[lo:lo + 16, :] = (m * sampled[y, lo:lo + 16, :]).astype(BF)
        joined[y + 1, 64:128, 0:COLS] = jnp.dot(
            wd[...], modulated[...], preferred_element_type=F32).astype(BF)
        return 0

    rows_loop(2, ROWS - 2, aligned_row)

    def edge4(fn):
        return lambda i, c: fn(i + (i // 2) * (ROWS - 4), c)

    def ring4(fn):
        return lambda i, c: fn(i - 1 + (i // 2) * (ROWS - 2), c)

    row_in(S_H1_IN, h1, 2, 1)
    row_in(S_H1, h1, 2, 0)
    rows_loop(0, 4, ring4(h2_row))
    rows_loop(0, 4, edge4(aligned_row))

    send(S_AL, UP, joined.at[1, 64:128, 0:COLS], joined.at[ROWS + 1, 64:128, 0:COLS])
    send(S_AL, DOWN, joined.at[ROWS, 64:128, 0:COLS], joined.at[0, 64:128, 0:COLS])
    pack_al[0] = pack_tiles(
        [joined[y + 1, 64:128, 0:BLK].astype(F32) for y in range(ROWS)], 0).astype(BF)
    pack_al[1] = pack_tiles(
        [joined[y + 1, 64:128, COLS - BLK:COLS].astype(F32) for y in range(ROWS)], 1).astype(BF)
    for side, dirs in ((0, (LEFT, UL, DL)), (1, (RIGHT, UR, DR))):
        for d in dirs:
            send(S_ALM, d, pack_al.at[side], got_al.at[OPP[d]])

    def margins(kind, got, lo):
        for d in range(8):
            if d not in (UP, DOWN):
                wait_recv(kind, d, got.at[d])

        def put(i, from_right, from_left, y):
            joined[i, lo:lo + 64, COLS:WIDE] = unpack(
                got[from_right].astype(F32), got[from_left].astype(F32), y).astype(BF)

        for y in range(ROWS):
            put(y + 1, RIGHT, LEFT, y)
        put(0, UR, UL, ROWS - 1)
        put(ROWS + 1, DR, DL, 0)

    margins(S_CURM, got_cur, 0)
    margins(S_ALM, got_al, 64)

    def t0_row(y, _):
        t0[y + 2] = leaky(conv_row(joined, y, wg[...])).astype(BF)
        return 0

    def inner_row(dst, src, r):
        def go(y, _):
            v = jnp.maximum(conv_row(src, y + 1, wr[r]), 0.0)
            dst[y + 1] = jnp.where(in_frame(y), v, 0.0).astype(BF)
            return 0
        return go

    def t1_row(y, _):
        t1[y + 2] = (t0[y + 2].astype(F32) + conv_row(i0, y, wr[1])).astype(BF)
        return 0

    def final_row(y, _):
        trunk = (t1[y + 2].astype(F32) + conv_row(i1, y, wr[3])).astype(BF)
        trunk = trunk[:, 0:COLS].astype(F32)
        out_ref[y] = (trunk + joined[y + 1, 64:128, 0:COLS].astype(F32)).astype(BF)
        return 0

    t0_row(1, 0)
    t0_row(ROWS - 2, 0)
    row_out(S_T0_IN, t0, 2, 1)
    rows_loop(2, ROWS - 2, t0_row)
    wait_recv(S_CUR, UP, joined.at[0, 0:64, 0:COLS])
    wait_recv(S_CUR, DOWN, joined.at[ROWS + 1, 0:64, 0:COLS])
    wait_recv(S_AL, UP, joined.at[0, 64:128, 0:COLS])
    wait_recv(S_AL, DOWN, joined.at[ROWS + 1, 64:128, 0:COLS])
    t0_row(0, 0)
    t0_row(ROWS - 1, 0)
    row_out(S_T0, t0, 2, 0)
    inner0 = inner_row(i0, t0, 0)
    inner1 = inner_row(i1, t1, 2)
    rows_loop(1, ROWS - 1, inner0)
    rows_loop(2, ROWS - 2, t1_row)
    row_in(S_T0_IN, t0, 2, 1)
    row_in(S_T0, t0, 2, 0)
    rows_loop(0, 4, ring4(inner0))
    t1_row(0, 0)
    t1_row(ROWS - 1, 0)
    row_out(S_T1, t1, 2, 0)
    t1_row(1, 0)
    t1_row(ROWS - 2, 0)
    row_out(S_T1_IN, t1, 2, 1)
    rows_loop(1, ROWS - 1, inner1)
    rows_loop(2, ROWS - 2, final_row)
    row_in(S_T1, t1, 2, 0)
    inner1(0, 0)
    inner1(ROWS - 1, 0)
    final_row(1, 0)
    final_row(ROWS - 2, 0)
    row_in(S_T1_IN, t1, 2, 1)
    inner1(-1, 0)
    inner1(ROWS, 0)
    final_row(0, 0)
    final_row(ROWS - 1, 0)

    wait_send(S_OFF, LEFT, pack_off.at[0])
    wait_send(S_OFF, RIGHT, pack_off.at[1])
    wait_send(S_SRC, UP, w_lat_up)
    wait_send(S_SRC, DOWN, w_lat_dn)
    wait_send(S_SRC, LEFT, w_left)
    wait_send(S_SRC, RIGHT, w_right)

    def relay_sent(kind, rows):
        wait_send(kind, LEFT, win.at[rows, 2:4])
        wait_send(kind, RIGHT, win.at[rows, 4:6])

    pl.when(has_up)(lambda: relay_sent(S_SRC_LO, slice(0, 2)))
    pl.when(has_down)(lambda: relay_sent(S_SRC_HI, slice(10, 12)))
    wait_send(S_PART, UP, part_out.at[0])
    wait_send(S_PART, DOWN, part_out.at[1])
    for side, dirs in ((0, (LEFT, UL, DL)), (1, (RIGHT, UR, DR))):
        for d in dirs:
            wait_send(S_CURM, d, pack_cur.at[side])
            wait_send(S_ALM, d, pack_al.at[side])
    wait_send(S_CUR, UP, joined.at[1, 0:64, 0:COLS])
    wait_send(S_CUR, DOWN, joined.at[ROWS, 0:64, 0:COLS])
    wait_send(S_AL, UP, joined.at[1, 64:128, 0:COLS])
    wait_send(S_AL, DOWN, joined.at[ROWS, 64:128, 0:COLS])
    for kind, buf in ((S_H1, h1), (S_T0, t0), (S_T1, t1)):
        row_sent(kind, buf, 2, 0)
        row_sent(kind + 1, buf, 2, 1)


def shards(
    offset_input, current, source, first_weight, second_weight, mask_weight, deform_weight,
    merge_weight, residual_weight, footprint, tile_scale, hats,
):
    n_lon, n_lat = lax.axis_size("lon"), lax.axis_size("lat")
    assert n_lon & (n_lon - 1) == 0
    vmem = pl.BlockSpec(memory_space=pltpu.VMEM)
    smem = pl.BlockSpec(memory_space=pltpu.SMEM)
    hbm = pl.BlockSpec(memory_space=pl.ANY)
    V = pltpu.VMEM
    out = pl.pallas_call(
        functools.partial(kernel, n_lon, n_lat),
        out_shape=jax.ShapeDtypeStruct((ROWS, 64, COLS), BF),
        in_specs=[hbm] * 9 + [smem, smem, hbm],
        out_specs=vmem,
        scratch_shapes=[
            V((9, 64, CIN), BF), V((9, 64, 64), BF), V((9, 64, 144), BF), V((9, 64, 64), BF),
            V((9, 64, 128), BF), V((4, 9, 64, 64), BF),
            V((CIN * ROWS, COLS), BF), V((64 * ROWS, COLS), BF), V((64 * ROWS, COLS), BF),
            V((NB, CIN * ROWS, BLK), F32),
            V((NB, 64 * ROWS, BLK), F32),
            V((ROWS, NB * K2 * BLK, BLK), BF),
            V((WIN_ROWS, WIN_COLS, 64, BLK), BF),
            V((ROWS, TAPS * 64, COLS), F32),
            V((TAPS * 64, COLS), BF),
            V((ROWS + 2, CPAD, WIDE), BF),
            V((ROWS + 4, 64, WIDE), BF),
            V((ROWS + 2, 192, WIDE), BF),
            V((ROWS + 2, 128, WIDE), BF),
            V((ROWS + 4, 64, WIDE), BF),
            V((ROWS + 2, 64, WIDE), BF),
            V((ROWS + 4, 64, WIDE), BF),
            V((ROWS + 2, 64, WIDE), BF),
            V((192, 3 * CPAD), BF), V((192, 192), BF), V((144, 576), BF), V((64, 576), BF),
            V((192, 384), BF), V((4, 192, 192), BF),
            V((2, 208, BLK), BF), V((2, 208, BLK), BF),
            V((2, 64, BLK), BF), V((8, 64, BLK), BF),
            V((2, 64, BLK), BF), V((8, 64, BLK), BF),
            V((2, 64, WIDE), BF), V((2, 64, WIDE), BF), V((2, 64, WIDE), F32),
            pltpu.SemaphoreType.DMA((9,)),
            pltpu.SemaphoreType.DMA((ROWS,)),
            pltpu.SemaphoreType.DMA((15, 8)),
            pltpu.SemaphoreType.DMA((15, 8)),
        ],
        compiler_params=pltpu.CompilerParams(
            collective_id=0, has_side_effects=True, vmem_limit_bytes=60 * 2**20),
    )(
        offset_input.reshape(CIN * ROWS, COLS),
        current.reshape(64 * ROWS, COLS),
        source.reshape(64 * ROWS, COLS),
        first_weight, second_weight, mask_weight.transpose(0, 2, 1), deform_weight, merge_weight,
        residual_weight.reshape(4, 9, 64, 64),
        footprint.transpose(0, 1, 3, 2), tile_scale.transpose(0, 1, 3, 2),
        hats.reshape(ROWS, NB * K2 * BLK, BLK),
    )
    return out.transpose(1, 0, 2)


def solution(mesh):
    in_specs = (
        P(None, "lat", "lon"),
        P(None, "lat", "lon"),
        P(None, "lat", "lon"),
        P(),
        P(),
        P(),
        P(),
        P(),
        P(),
        P("lat", "lon", None, None),
        P("lat", "lon", None, None),
        P("lat", "lon", None, None, None, None),
    )
    return jax.shard_map(
        shards, mesh=mesh, in_specs=in_specs, out_specs=P(None, "lat", "lon"), check_vma=False)
```

```python
import functools

import jax
import jax.numpy as jnp
from jax import lax
from jax.experimental import pallas as pl
from jax.experimental.pallas import tpu as pltpu
from jax.sharding import PartitionSpec as P

BF = jnp.bfloat16
F32 = jnp.float32
MESH = pl.DeviceIdType.MESH

BLK = 128
ROWS = 8
COLS = 512
WIDE = 640
CIN = 196
CPAD = 256
NB = COLS // BLK
WIN_ROWS = ROWS + 4
WIN_COLS = NB + 4
TAPS = 9
K2 = 18

LEFT, RIGHT, UP, DOWN, UL, UR, DL, DR = range(8)
OPP = (RIGHT, LEFT, DOWN, UP, DR, DL, UR, UL)
(S_OFF, S_SRC, S_SRC_LO, S_SRC_HI, S_CURM, S_CUR, S_PART, S_H1, S_H1_IN, S_ALM, S_AL,
 S_T0, S_T0_IN, S_T1, S_T1_IN) = range(15)


def leaky(v):
    return jnp.where(v > 0, v, 0.1 * v)


def kernel(
    n_lon, n_lat,
    off_hbm, cur_hbm, src_hbm, w1_hbm, w2_hbm, wm_hbm, wd_hbm, wg_hbm, wr_hbm,
    foot_hbm, scale_hbm, hats_hbm, out_hbm,
    foot_ref, scale_ref, out_ref,
    w1_ref, w2_ref, wm_ref, wd_ref, wg_ref, wr_ref,
    raw_off, raw_src, raw_cur, stage, stage2, hats, near, win, sampled, modulated,
    v0, h1, h2, joined, t0, i0, t1, i1,
    w1, w2, wm, wd, wg, wr,
    pack_off, got_off, pack_cur, got_cur, pack_al, got_al,
    part_out, part_in, part_own,
    load_sem, hat_sem, out_sem, send_sem, recv_sem,
):
    lon = lax.axis_index("lon")
    lat = lax.axis_index("lat")
    left = lax.rem(lon + n_lon - 1, n_lon)
    right = lax.rem(lon + 1, n_lon)
    has_up = lat > 0
    has_down = lat < n_lat - 1
    nb = {
        LEFT: (None, (left, lat)), RIGHT: (None, (right, lat)),
        UP: (has_up, (lon, lat - 1)), DOWN: (has_down, (lon, lat + 1)),
        UL: (has_up, (left, lat - 1)), UR: (has_up, (right, lat - 1)),
        DL: (has_down, (left, lat + 1)), DR: (has_down, (right, lat + 1)),
    }

    def guarded(cond, fn):
        if cond is None:
            fn()
        else:
            pl.when(cond)(fn)

    def copy(kind, direction, src, dst):
        return pltpu.make_async_remote_copy(
            src_ref=src, dst_ref=dst,
            send_sem=send_sem.at[kind, direction],
            recv_sem=recv_sem.at[kind, OPP[direction]],
            device_id=nb[direction][1], device_id_type=MESH,
        )

    def send(kind, direction, src, dst):
        guarded(nb[direction][0], lambda: copy(kind, direction, src, dst).start())

    def wait_send(kind, direction, src):
        def go():
            pltpu.make_async_remote_copy(
                src_ref=src, dst_ref=src, send_sem=send_sem.at[kind, direction],
                recv_sem=recv_sem.at[kind, direction],
                device_id=nb[direction][1], device_id_type=MESH,
            ).wait_send()
        guarded(nb[direction][0], go)

    def wait_recv(kind, direction, dst):
        def go():
            pltpu.make_async_remote_copy(
                src_ref=dst, dst_ref=dst, send_sem=send_sem.at[kind, direction],
                recv_sem=recv_sem.at[kind, direction],
                device_id=nb[direction][1], device_id_type=MESH,
            ).wait_recv()
        guarded(nb[direction][0], go)

    load_off = pltpu.make_async_copy(off_hbm, raw_off, load_sem.at[0])
    load_src = pltpu.make_async_copy(src_hbm, raw_src, load_sem.at[1])
    load_cur = pltpu.make_async_copy(cur_hbm, raw_cur, load_sem.at[2])
    load_off.start()
    load_src.start()
    load_weights = [
        pltpu.make_async_copy(a, b, load_sem.at[3 + n])
        for n, (a, b) in enumerate((
            (w1_hbm, w1_ref), (w2_hbm, w2_ref), (wm_hbm, wm_ref), (wd_hbm, wd_ref),
            (wg_hbm, wg_ref), (wr_hbm, wr_ref), (foot_hbm, foot_ref), (scale_hbm, scale_ref)))
    ]
    for load in load_weights:
        load.start()
    load_cur.start()

    def hat_load(y):
        return pltpu.make_async_copy(hats_hbm.at[y], hats.at[y], hat_sem.at[y])

    for y in range(ROWS):
        hat_load(y).start()

    def zero_rows(buf, lo, hi):
        buf[lo:hi] = jnp.zeros((hi - lo,) + buf.shape[1:], buf.dtype)

    def no_halo(top):
        for buf, m in ((h1, 2), (joined, 1), (t0, 2), (t1, 2)):
            if top:
                zero_rows(buf, 0, m)
            else:
                zero_rows(buf, ROWS + m, ROWS + 2 * m)
        n = 0 if top else 1
        zero_rows(part_in, n, n + 1)
        for d in (UL, UR) if top else (DL, DR):
            zero_rows(got_cur, d, d + 1)
            zero_rows(got_al, d, d + 1)

    pl.when(jnp.logical_not(has_up))(lambda: no_halo(True))
    pl.when(jnp.logical_not(has_down))(lambda: no_halo(False))

    barrier = pltpu.get_barrier_semaphore()
    for d in range(8):
        guarded(nb[d][0], lambda d=d: pl.semaphore_signal(
            barrier, inc=1, device_id=nb[d][1], device_id_type=MESH))

    def all_here():
        both = has_up & has_down
        pl.when(both)(lambda: pl.semaphore_wait(barrier, 8))
        pl.when(jnp.logical_not(both))(lambda: pl.semaphore_wait(barrier, 5))

    zero_rows(v0, 0, 1)
    zero_rows(v0, ROWS + 1, ROWS + 2)
    pack_off[...] = jnp.zeros(pack_off.shape, BF)
    for i in range(1, ROWS + 1):
        v0[i, 192:CPAD, :] = jnp.zeros((CPAD - 192, WIDE), BF)

    lane = lax.broadcasted_iota(jnp.int32, (1, BLK), 1)

    def pack_tiles(tiles, side):
        total = None
        for y, tile in enumerate(tiles):
            shift = 8 * y if side == 0 else 8 * y + 8
            moved = pltpu.roll(tile, shift, 1) if shift else tile
            here = (lane >= 8 * y) & (lane < 8 * y + 8)
            total = jnp.where(here, moved, 0.0 if total is None else total)
        return total

    def unpack(from_right, from_left, y):
        a = pltpu.roll(from_right, (128 - 8 * y) % 128, 1) if y else from_right
        b = pltpu.roll(from_left, 120 - 8 * y, 1)
        return jnp.where(lane < 8, a, jnp.where(lane >= 120, b, 0.0))

    load_off.wait()
    def stage_off(j):
        stage[j] = raw_off[:, j * BLK:(j + 1) * BLK].astype(F32)

    stage_off(0)
    stage_off(NB - 1)

    def staged(channels, y, j):
        return stage[j, pl.ds(y, channels, stride=ROWS), :]

    pack_off[0, 0:CIN, :] = pack_tiles(
        [staged(CIN, y, 0) for y in range(ROWS)], 0).astype(BF)
    pack_off[1, 0:CIN, :] = pack_tiles(
        [staged(CIN, y, NB - 1) for y in range(ROWS)], 1).astype(BF)
    all_here()
    send(S_OFF, LEFT, pack_off.at[0], got_off.at[0])
    send(S_OFF, RIGHT, pack_off.at[1], got_off.at[1])

    load_src.wait()
    for j in range(NB):
        stage2[j] = raw_src[:, j * BLK:(j + 1) * BLK].astype(F32)

    def win_row(y, _):
        for k in range(4):
            for j in range(NB):
                near[y, j + 2, k * 16:(k + 1) * 16, :] = stage2[
                    j, pl.ds(k * ROWS + y, 16, stride=4 * ROWS), :].astype(BF)
        return 0

    lax.fori_loop(0, ROWS, win_row, 0)

    def by_reach(row_tile, fn):
        outer = (row_tile < n_lat // 4) | (row_tile >= n_lat - n_lat // 4)
        pl.when(outer)(lambda: fn(2))
        pl.when(jnp.logical_not(outer))(lambda: fn(1))

    def to_left(rows, n, buf=win):
        return buf.at[rows, 2:2 + n]

    def to_right(rows, n, buf=win):
        return buf.at[rows, 6 - n:6]

    def from_left(rows, n, buf=win):
        return buf.at[rows, 2 - n:2]

    def from_right(rows, n, buf=win):
        return buf.at[rows, 6:6 + n]

    INNER, TOP, BOTTOM = slice(0, 8), slice(0, 2), slice(10, 12)
    FIRST, LAST = slice(0, 2), slice(6, 8)
    odd = lax.rem(lon, 2) == 1
    even = jnp.logical_not(odd)

    def source_columns(n):
        send(S_SRC, LEFT, to_left(INNER, n, near), from_right(INNER, n, near))
        send(S_SRC, RIGHT, to_right(INNER, n, near), from_left(INNER, n, near))

    def source_columns_in(n):
        wait_recv(S_SRC, RIGHT, from_right(INNER, n, near))
        wait_recv(S_SRC, LEFT, from_left(INNER, n, near))

    def source_columns_sent(n):
        wait_send(S_SRC, LEFT, to_left(INNER, n, near))
        wait_send(S_SRC, RIGHT, to_right(INNER, n, near))

    def source_rows():
        send(S_SRC, UP, near.at[FIRST, 2:6], win.at[BOTTOM, 2:6])
        send(S_SRC, DOWN, near.at[LAST, 2:6], win.at[TOP, 2:6])

        @pl.when(even)
        def _():
            by_reach(lat - 1, lambda n: send(S_SRC, UL, to_left(FIRST, n, near), from_right(BOTTOM, n)))
            by_reach(lat + 1, lambda n: send(S_SRC, DL, to_left(LAST, n, near), from_right(TOP, n)))

        @pl.when(odd)
        def _():
            by_reach(lat - 1, lambda n: send(S_SRC, UR, to_right(FIRST, n, near), from_left(BOTTOM, n)))
            by_reach(lat + 1, lambda n: send(S_SRC, DR, to_right(LAST, n, near), from_left(TOP, n)))

    def source_rows_sent():
        wait_send(S_SRC, UP, near.at[FIRST, 2:6])
        wait_send(S_SRC, DOWN, near.at[LAST, 2:6])

        @pl.when(even)
        def _():
            by_reach(lat - 1, lambda n: wait_send(S_SRC, UL, to_left(FIRST, n, near)))
            by_reach(lat + 1, lambda n: wait_send(S_SRC, DL, to_left(LAST, n, near)))

        @pl.when(odd)
        def _():
            by_reach(lat - 1, lambda n: wait_send(S_SRC, UR, to_right(FIRST, n, near)))
            by_reach(lat + 1, lambda n: wait_send(S_SRC, DR, to_right(LAST, n, near)))

    def relay(kind, rows, n):
        pl.when(even)(lambda: send(kind, RIGHT, to_right(rows, n), from_left(rows, n)))
        pl.when(odd)(lambda: send(kind, LEFT, to_left(rows, n), from_right(rows, n)))

    def relay_in(kind, rows, n):
        pl.when(even)(lambda: wait_recv(kind, RIGHT, from_right(rows, n)))
        pl.when(odd)(lambda: wait_recv(kind, LEFT, from_left(rows, n)))

    def relay_sent(kind, rows, n):
        pl.when(even)(lambda: wait_send(kind, RIGHT, to_right(rows, n)))
        pl.when(odd)(lambda: wait_send(kind, LEFT, to_left(rows, n)))

    def each_relay(fn):
        pl.when(has_up)(lambda: by_reach(lat, lambda n: fn(S_SRC_LO, TOP, n)))
        pl.when(has_down)(lambda: by_reach(lat, lambda n: fn(S_SRC_HI, BOTTOM, n)))

    def source_rows_in():
        wait_recv(S_SRC, UP, win.at[TOP, 2:6])
        wait_recv(S_SRC, DOWN, win.at[BOTTOM, 2:6])
        each_relay(relay)

    def source_corners_in():
        @pl.when(odd)
        def _():
            by_reach(lat, lambda n: wait_recv(S_SRC, UR, from_right(TOP, n)))
            by_reach(lat, lambda n: wait_recv(S_SRC, DR, from_right(BOTTOM, n)))

        @pl.when(even)
        def _():
            by_reach(lat, lambda n: wait_recv(S_SRC, UL, from_left(TOP, n)))
            by_reach(lat, lambda n: wait_recv(S_SRC, DL, from_left(BOTTOM, n)))

        each_relay(relay_in)

    by_reach(lat, source_columns)

    for j in range(1, NB - 1):
        stage_off(j)

    def v0_row(y, _):
        for j in range(NB):
            v0[y + 1, 0:CIN, j * BLK:(j + 1) * BLK] = staged(CIN, y, j).astype(BF)
        return 0

    lax.fori_loop(0, ROWS, v0_row, 0)

    load_cur.wait()
    for j in range(NB):
        stage2[j] = raw_cur[:, j * BLK:(j + 1) * BLK].astype(F32)

    def cur_staged(y, j):
        return stage2[j, pl.ds(y, 64, stride=ROWS), :]

    def cur_row(y, _):
        for j in range(NB):
            joined[y + 1, 0:64, j * BLK:(j + 1) * BLK] = cur_staged(y, j).astype(BF)
        return 0

    lax.fori_loop(0, ROWS, cur_row, 0)
    pack_cur[0] = pack_tiles([cur_staged(y, 0) for y in range(ROWS)], 0).astype(BF)
    pack_cur[1] = pack_tiles([cur_staged(y, NB - 1) for y in range(ROWS)], 1).astype(BF)

    for load in load_weights:
        load.wait()
    w1[...] = jnp.zeros(w1.shape, BF)
    for a in range(3):
        for b in range(3):
            w1[b * 64:(b + 1) * 64, a * CPAD:a * CPAD + CIN] = w1_ref[3 * a + b]
            wg[b * 64:(b + 1) * 64, a * 128:(a + 1) * 128] = wg_ref[3 * a + b]
    for b in range(3):
        w2[b * 64:(b + 1) * 64, :] = jnp.concatenate([w2_ref[3 * a + b] for a in range(3)], axis=1)
        for r in range(4):
            wr[r, b * 64:(b + 1) * 64, :] = jnp.concatenate(
                [wr_ref[r, 3 * a + b] for a in range(3)], axis=1)
    wm[...] = wm_ref[...].reshape(TAPS * 64, 144).astype(F32).T.astype(BF)
    row_id = lax.broadcasted_iota(jnp.int32, (64, 64), 0)
    col_id = lax.broadcasted_iota(jnp.int32, (64, 64), 1)
    perm = (row_id == (col_id % 16) * 4 + col_id // 16).astype(BF)
    wd[...] = jnp.concatenate(
        [jnp.dot(wd_ref[t], perm, preferred_element_type=F32).astype(BF) for t in range(TAPS)], axis=1)

    def spread(p):
        n = p.shape[1]
        return pltpu.roll(p[0:64], 1, 1) + p[64:128] + pltpu.roll(p[128:192], n - 1, 1)

    def conv_row(src, i, weight):
        x = src[pl.ds(i, 3)].reshape(3 * src.shape[1], WIDE)
        return spread(jnp.dot(weight, x, preferred_element_type=F32))

    def row_out(kind, buf, m, n):
        send(kind, UP, buf.at[m + n], buf.at[ROWS + m + n])
        send(kind, DOWN, buf.at[ROWS + m - 1 - n], buf.at[m - 1 - n])

    def row_in(kind, buf, m, n):
        wait_recv(kind, UP, buf.at[m - 1 - n])
        wait_recv(kind, DOWN, buf.at[ROWS + m + n])

    def row_sent(kind, buf, m, n):
        wait_send(kind, UP, buf.at[m + n])
        wait_send(kind, DOWN, buf.at[ROWS + m - 1 - n])

    def rows_loop(lo, hi, fn):
        lax.fori_loop(lo, hi, fn, 0, unroll=True)

    def edge4(fn):
        return lambda i, c: fn(i + (i // 2) * (ROWS - 4), c)

    def ring4(fn):
        return lambda i, c: fn(i - 1 + (i // 2) * (ROWS - 2), c)

    wait_recv(S_OFF, RIGHT, got_off.at[0])
    wait_recv(S_OFF, LEFT, got_off.at[1])
    for y in range(ROWS):
        v0[y + 1, 0:CIN, COLS:WIDE] = unpack(
            got_off[0, 0:CIN, :].astype(F32), got_off[1, 0:CIN, :].astype(F32), y).astype(BF)
    part_out[0] = spread(jnp.dot(w1[:, 2 * CPAD:], v0[1], preferred_element_type=F32)).astype(BF)
    part_out[1] = spread(jnp.dot(w1[:, :CPAD], v0[ROWS], preferred_element_type=F32)).astype(BF)
    send(S_PART, UP, part_out.at[0], part_in.at[1])
    send(S_PART, DOWN, part_out.at[1], part_in.at[0])
    source_rows()

    def h1_row(y, _):
        h1[y + 2] = leaky(conv_row(v0, y, w1[...])).astype(BF)
        return 0

    h1_row(1, 0)
    h1_row(ROWS - 2, 0)
    row_out(S_H1_IN, h1, 2, 1)
    rows_loop(2, ROWS - 2, h1_row)
    part_own[0] = conv_row(v0, 0, w1[...])
    part_own[1] = conv_row(v0, ROWS - 1, w1[...])

    total = NB * n_lon
    shift = total.bit_length() - 1
    col_base = lon * NB - 2

    def sample_row(y, src, first, count):
        for j in range(NB):
            for t in range(TAPS):
                parts = []
                for f in range(2):
                    ix = foot_ref[y, j, f, t]
                    row = jnp.clip(lax.shift_right_logical(ix, shift) - first, 0, count - 1)
                    col = jnp.minimum(lax.bitwise_and(ix - col_base, total - 1), WIN_COLS - 1)
                    parts.append((src[row, col].astype(F32) * scale_ref[y, j, f, t]).astype(BF))
                tile = hats[y, (j * K2 + 2 * t) * BLK:(j * K2 + 2 * t + 2) * BLK, :]
                sampled[y, t * 64:(t + 1) * 64, j * BLK:(j + 1) * BLK] = jnp.dot(
                    jnp.concatenate(parts, axis=1), tile, preferred_element_type=F32)
        return 0

    by_reach(lat, source_columns_in)
    for y in range(2, ROWS - 2):
        hat_load(y).wait()
    rows_loop(2, ROWS - 2, lambda y, _: sample_row(y, near, lat * ROWS, ROWS))
    win[2:2 + ROWS] = near[...]

    wait_recv(S_PART, UP, part_in.at[0])
    wait_recv(S_PART, DOWN, part_in.at[1])
    h1[2] = leaky(part_own[0] + part_in[0].astype(F32)).astype(BF)
    h1[ROWS + 1] = leaky(part_own[1] + part_in[1].astype(F32)).astype(BF)

    row_out(S_H1, h1, 2, 0)

    for side, dirs in ((0, (LEFT, UL, DL)), (1, (RIGHT, UR, DR))):
        for d in dirs:
            send(S_CURM, d, pack_cur.at[side], got_cur.at[OPP[d]])
    send(S_CUR, UP, joined.at[1, 0:64, 0:COLS], joined.at[ROWS + 1, 0:64, 0:COLS])
    send(S_CUR, DOWN, joined.at[ROWS, 0:64, 0:COLS], joined.at[0, 0:64, 0:COLS])

    def in_frame(y):
        g = lat * ROWS + y
        return (g >= 0) & (g < n_lat * ROWS)

    def h2_row(y, _):
        v = leaky(conv_row(h1, y + 1, w2[...]))
        v = jnp.where(in_frame(y), v, 0.0)
        h2[y + 1, 0:64] = pltpu.roll(v, 1, 1).astype(BF)
        h2[y + 1, 64:128] = v.astype(BF)
        h2[y + 1, 128:192] = pltpu.roll(v, WIDE - 1, 1).astype(BF)
        return 0

    rows_loop(1, ROWS - 1, h2_row)

    source_rows_in()
    source_corners_in()
    for y in (0, 1, ROWS - 2, ROWS - 1):
        hat_load(y).wait()
    rows_loop(0, 4, edge4(lambda y, _: sample_row(y, win, lat * ROWS - 2, WIN_ROWS)))

    def aligned_row(y, _):
        x = h2[pl.ds(y, 3)].reshape(576, WIDE)[:, 0:COLS]
        logits = jnp.dot(wm[...], x, preferred_element_type=F32)
        mod = 1.0 / (1.0 + jnp.exp(-logits))
        for t in range(TAPS):
            m = mod[t * 16:(t + 1) * 16]
            for k in range(4):
                lo = t * 64 + k * 16
                modulated[lo:lo + 16, :] = (m * sampled[y, lo:lo + 16, :]).astype(BF)
        joined[y + 1, 64:128, 0:COLS] = jnp.dot(
            wd[...], modulated[...], preferred_element_type=F32).astype(BF)
        return 0

    rows_loop(2, ROWS - 2, aligned_row)

    row_in(S_H1_IN, h1, 2, 1)
    row_in(S_H1, h1, 2, 0)
    rows_loop(0, 4, ring4(h2_row))
    rows_loop(0, 4, edge4(aligned_row))

    send(S_AL, UP, joined.at[1, 64:128, 0:COLS], joined.at[ROWS + 1, 64:128, 0:COLS])
    send(S_AL, DOWN, joined.at[ROWS, 64:128, 0:COLS], joined.at[0, 64:128, 0:COLS])
    pack_al[0] = pack_tiles(
        [joined[y + 1, 64:128, 0:BLK].astype(F32) for y in range(ROWS)], 0).astype(BF)
    pack_al[1] = pack_tiles(
        [joined[y + 1, 64:128, COLS - BLK:COLS].astype(F32) for y in range(ROWS)], 1).astype(BF)
    for side, dirs in ((0, (LEFT, UL, DL)), (1, (RIGHT, UR, DR))):
        for d in dirs:
            send(S_ALM, d, pack_al.at[side], got_al.at[OPP[d]])

    def margins(kind, got, lo):
        for d in range(8):
            if d not in (UP, DOWN):
                wait_recv(kind, d, got.at[d])

        def put(i, from_right, from_left, y):
            joined[i, lo:lo + 64, COLS:WIDE] = unpack(
                got[from_right].astype(F32), got[from_left].astype(F32), y).astype(BF)

        for y in range(ROWS):
            put(y + 1, RIGHT, LEFT, y)
        put(0, UR, UL, ROWS - 1)
        put(ROWS + 1, DR, DL, 0)

    margins(S_CURM, got_cur, 0)
    margins(S_ALM, got_al, 64)

    def t0_row(y, _):
        t0[y + 2] = leaky(conv_row(joined, y, wg[...])).astype(BF)
        return 0

    def inner_row(dst, src, r):
        def go(y, _):
            v = jnp.maximum(conv_row(src, y + 1, wr[r]), 0.0)
            dst[y + 1] = jnp.where(in_frame(y), v, 0.0).astype(BF)
            return 0
        return go

    def t1_row(y, _):
        t1[y + 2] = (t0[y + 2].astype(F32) + conv_row(i0, y, wr[1])).astype(BF)
        return 0

    def out_copy(y):
        return pltpu.make_async_copy(out_ref.at[y], out_hbm.at[y], out_sem.at[y])

    def final_row(y, _):
        trunk = (t1[y + 2].astype(F32) + conv_row(i1, y, wr[3])).astype(BF)
        trunk = trunk[:, 0:COLS].astype(F32)
        out_ref[y] = (trunk + joined[y + 1, 64:128, 0:COLS].astype(F32)).astype(BF)
        out_copy(y).start()
        return 0

    t0_row(1, 0)
    t0_row(ROWS - 2, 0)
    row_out(S_T0_IN, t0, 2, 1)
    rows_loop(2, ROWS - 2, t0_row)
    wait_recv(S_CUR, UP, joined.at[0, 0:64, 0:COLS])
    wait_recv(S_CUR, DOWN, joined.at[ROWS + 1, 0:64, 0:COLS])
    wait_recv(S_AL, UP, joined.at[0, 64:128, 0:COLS])
    wait_recv(S_AL, DOWN, joined.at[ROWS + 1, 64:128, 0:COLS])
    t0_row(0, 0)
    t0_row(ROWS - 1, 0)
    row_out(S_T0, t0, 2, 0)
    inner0 = inner_row(i0, t0, 0)
    inner1 = inner_row(i1, t1, 2)
    rows_loop(1, ROWS - 1, inner0)
    rows_loop(2, ROWS - 2, t1_row)
    row_in(S_T0_IN, t0, 2, 1)
    row_in(S_T0, t0, 2, 0)
    rows_loop(0, 4, ring4(inner0))
    t1_row(0, 0)
    t1_row(ROWS - 1, 0)
    row_out(S_T1, t1, 2, 0)
    t1_row(1, 0)
    t1_row(ROWS - 2, 0)
    row_out(S_T1_IN, t1, 2, 1)
    rows_loop(1, ROWS - 1, inner1)
    rows_loop(2, ROWS - 2, final_row)
    row_in(S_T1, t1, 2, 0)
    inner1(0, 0)
    inner1(ROWS - 1, 0)
    final_row(1, 0)
    final_row(ROWS - 2, 0)
    row_in(S_T1_IN, t1, 2, 1)
    inner1(-1, 0)
    inner1(ROWS, 0)
    final_row(0, 0)
    final_row(ROWS - 1, 0)

    for y in range(ROWS):
        out_copy(y).wait()
    wait_send(S_OFF, LEFT, pack_off.at[0])
    wait_send(S_OFF, RIGHT, pack_off.at[1])
    by_reach(lat, source_columns_sent)
    source_rows_sent()
    each_relay(relay_sent)
    wait_send(S_PART, UP, part_out.at[0])
    wait_send(S_PART, DOWN, part_out.at[1])
    for side, dirs in ((0, (LEFT, UL, DL)), (1, (RIGHT, UR, DR))):
        for d in dirs:
            wait_send(S_CURM, d, pack_cur.at[side])
            wait_send(S_ALM, d, pack_al.at[side])
    wait_send(S_CUR, UP, joined.at[1, 0:64, 0:COLS])
    wait_send(S_CUR, DOWN, joined.at[ROWS, 0:64, 0:COLS])
    wait_send(S_AL, UP, joined.at[1, 64:128, 0:COLS])
    wait_send(S_AL, DOWN, joined.at[ROWS, 64:128, 0:COLS])
    for kind, buf in ((S_H1, h1), (S_T0, t0), (S_T1, t1)):
        row_sent(kind, buf, 2, 0)
        row_sent(kind + 1, buf, 2, 1)


def shards(
    offset_input, current, source, first_weight, second_weight, mask_weight, deform_weight,
    merge_weight, residual_weight, footprint, tile_scale, hats,
):
    n_lon, n_lat = lax.axis_size("lon"), lax.axis_size("lat")
    assert n_lon & (n_lon - 1) == 0
    hbm = pl.BlockSpec(memory_space=pl.ANY)
    V = pltpu.VMEM
    out = pl.pallas_call(
        functools.partial(kernel, n_lon, n_lat),
        out_shape=jax.ShapeDtypeStruct((ROWS, 64, COLS), BF),
        in_specs=[hbm] * 12,
        out_specs=hbm,
        scratch_shapes=[
            pltpu.SMEM((ROWS, NB, 2, TAPS), jnp.int32), pltpu.SMEM((ROWS, NB, 2, TAPS), F32),
            V((ROWS, 64, COLS), BF),
            V((9, 64, CIN), BF), V((9, 64, 64), BF), V((9, 64, 144), BF), V((9, 64, 64), BF),
            V((9, 64, 128), BF), V((4, 9, 64, 64), BF),
            V((CIN * ROWS, COLS), BF), V((64 * ROWS, COLS), BF), V((64 * ROWS, COLS), BF),
            V((NB, CIN * ROWS, BLK), F32),
            V((NB, 64 * ROWS, BLK), F32),
            V((ROWS, NB * K2 * BLK, BLK), BF),
            V((ROWS, WIN_COLS, 64, BLK), BF),
            V((WIN_ROWS, WIN_COLS, 64, BLK), BF),
            V((ROWS, TAPS * 64, COLS), F32),
            V((TAPS * 64, COLS), BF),
            V((ROWS + 2, CPAD, WIDE), BF),
            V((ROWS + 4, 64, WIDE), BF),
            V((ROWS + 2, 192, WIDE), BF),
            V((ROWS + 2, 128, WIDE), BF),
            V((ROWS + 4, 64, WIDE), BF),
            V((ROWS + 2, 64, WIDE), BF),
            V((ROWS + 4, 64, WIDE), BF),
            V((ROWS + 2, 64, WIDE), BF),
            V((192, 3 * CPAD), BF), V((192, 192), BF), V((144, 576), BF), V((64, 576), BF),
            V((192, 384), BF), V((4, 192, 192), BF),
            V((2, 208, BLK), BF), V((2, 208, BLK), BF),
            V((2, 64, BLK), BF), V((8, 64, BLK), BF),
            V((2, 64, BLK), BF), V((8, 64, BLK), BF),
            V((2, 64, WIDE), BF), V((2, 64, WIDE), BF), V((2, 64, WIDE), F32),
            pltpu.SemaphoreType.DMA((11,)),
            pltpu.SemaphoreType.DMA((ROWS,)),
            pltpu.SemaphoreType.DMA((ROWS,)),
            pltpu.SemaphoreType.DMA((15, 8)),
            pltpu.SemaphoreType.DMA((15, 8)),
        ],
        compiler_params=pltpu.CompilerParams(
            collective_id=0, has_side_effects=True, vmem_limit_bytes=60 * 2**20),
    )(
        offset_input.reshape(CIN * ROWS, COLS),
        current.reshape(64 * ROWS, COLS),
        source.reshape(64 * ROWS, COLS),
        first_weight, second_weight, mask_weight.transpose(0, 2, 1), deform_weight, merge_weight,
        residual_weight.reshape(4, 9, 64, 64),
        footprint.transpose(0, 1, 3, 2), tile_scale.transpose(0, 1, 3, 2),
        hats.reshape(ROWS, NB * K2 * BLK, BLK),
    )
    return out.transpose(1, 0, 2)


def solution(mesh):
    in_specs = (
        P(None, "lat", "lon"),
        P(None, "lat", "lon"),
        P(None, "lat", "lon"),
        P(),
        P(),
        P(),
        P(),
        P(),
        P(),
        P("lat", "lon", None, None),
        P("lat", "lon", None, None),
        P("lat", "lon", None, None, None, None),
    )
    return jax.shard_map(
        shards, mesh=mesh, in_specs=in_specs, out_specs=P(None, "lat", "lon"), check_vma=False)
```

```python
import functools

import jax
import jax.numpy as jnp
from jax import lax
from jax.experimental import pallas as pl
from jax.experimental.pallas import tpu as pltpu
from jax.sharding import PartitionSpec as P

BF = jnp.bfloat16
F32 = jnp.float32
MESH = pl.DeviceIdType.MESH

BLK = 128
ROWS = 8
COLS = 512
WIDE = 640
CIN = 196
CPAD = 256
NB = COLS // BLK
WIN_ROWS = ROWS + 4
WIN_COLS = NB + 4
TAPS = 9
K2 = 18

LEFT, RIGHT, UP, DOWN, UL, UR, DL, DR = range(8)
AL_CORNERS = ((0, UL), (0, UR), (1, DL), (1, DR))
OPP = (RIGHT, LEFT, DOWN, UP, DR, DL, UR, UL)
(S_OFF, S_SRC, S_SRC_LO, S_SRC_HI, S_CURM, S_CUR, S_PART, S_H1, S_H1_IN, S_ALM, S_AL,
 S_T0, S_T0_IN, S_T1, S_T1_IN) = range(15)
KINDS = 15


def leaky(v):
    return jnp.where(v > 0, v, 0.1 * v)


def kernel(
    n_lon, n_lat,
    off_hbm, cur_hbm, src_hbm, w1_hbm, w2_hbm, wm_hbm, wd_hbm, wg_hbm, wr_hbm,
    foot_hbm, scale_hbm, hats_hbm, out_hbm,
    foot_ref, scale_ref, out_ref,
    w1_ref, w2_ref, wm_ref, wd_ref, wg_ref, wr_ref,
    raw_off, raw_src, raw_cur, stage, stage2, hats, near, win, sampled, modulated,
    v0, h1, h2, joined, t0, i0, t1, i1,
    w1, w2, wm, wd, wg, wr,
    pack_off, got_off, pack_cur, got_cur, pack_al, got_al, got_corner,
    part_out, part_in, part_own, sq_out, sq_in,
    load_sem, hat_sem, out_sem, send_sem, recv_sem,
):
    lon = lax.axis_index("lon")
    lat = lax.axis_index("lat")
    left = lax.rem(lon + n_lon - 1, n_lon)
    right = lax.rem(lon + 1, n_lon)
    has_up = lat > 0
    has_down = lat < n_lat - 1
    nb = {
        LEFT: (None, (left, lat)), RIGHT: (None, (right, lat)),
        UP: (has_up, (lon, lat - 1)), DOWN: (has_down, (lon, lat + 1)),
        UL: (has_up, (left, lat - 1)), UR: (has_up, (right, lat - 1)),
        DL: (has_down, (left, lat + 1)), DR: (has_down, (right, lat + 1)),
    }

    def guarded(cond, fn):
        if cond is None:
            fn()
        else:
            pl.when(cond)(fn)

    def copy(kind, direction, src, dst):
        return pltpu.make_async_remote_copy(
            src_ref=src, dst_ref=dst,
            send_sem=send_sem.at[kind, direction],
            recv_sem=recv_sem.at[kind, OPP[direction]],
            device_id=nb[direction][1], device_id_type=MESH,
        )

    def send(kind, direction, src, dst):
        guarded(nb[direction][0], lambda: copy(kind, direction, src, dst).start())

    def wait_send(kind, direction, src):
        def go():
            pltpu.make_async_remote_copy(
                src_ref=src, dst_ref=src, send_sem=send_sem.at[kind, direction],
                recv_sem=recv_sem.at[kind, direction],
                device_id=nb[direction][1], device_id_type=MESH,
            ).wait_send()
        guarded(nb[direction][0], go)

    def wait_recv(kind, direction, dst):
        def go():
            pltpu.make_async_remote_copy(
                src_ref=dst, dst_ref=dst, send_sem=send_sem.at[kind, direction],
                recv_sem=recv_sem.at[kind, direction],
                device_id=nb[direction][1], device_id_type=MESH,
            ).wait_recv()
        guarded(nb[direction][0], go)

    barrier = pltpu.get_barrier_semaphore()
    for d in range(8):
        guarded(nb[d][0], lambda d=d: pl.semaphore_signal(
            barrier, inc=1, device_id=nb[d][1], device_id_type=MESH))

    def off_load(lo, hi, n):
        return pltpu.make_async_copy(off_hbm.at[:, lo:hi], raw_off.at[:, lo:hi], load_sem.at[n])

    load_off = [off_load(0, BLK, 0), off_load(COLS - BLK, COLS, 11), off_load(BLK, COLS - BLK, 12)]
    load_src = pltpu.make_async_copy(src_hbm, raw_src, load_sem.at[1])
    load_cur = pltpu.make_async_copy(cur_hbm, raw_cur, load_sem.at[2])
    for load in load_off:
        load.start()
    load_src.start()
    load_weights = [
        pltpu.make_async_copy(a, b, load_sem.at[3 + n])
        for n, (a, b) in enumerate((
            (w1_hbm, w1_ref), (w2_hbm, w2_ref), (wm_hbm, wm_ref), (wd_hbm, wd_ref),
            (wg_hbm, wg_ref), (wr_hbm, wr_ref), (foot_hbm, foot_ref), (scale_hbm, scale_ref)))
    ]
    for load in load_weights:
        load.start()
    load_cur.start()

    def hat_load(y):
        return pltpu.make_async_copy(hats_hbm.at[y], hats.at[y], hat_sem.at[y])

    def zero_rows(buf, lo, hi):
        buf[lo:hi] = jnp.zeros((hi - lo,) + buf.shape[1:], buf.dtype)

    def no_halo(top):
        for buf, m in ((h1, 2), (joined, 1), (t0, 2), (t1, 2)):
            if top:
                zero_rows(buf, 0, m)
            else:
                zero_rows(buf, ROWS + m, ROWS + 2 * m)
        n = 0 if top else 1
        zero_rows(part_in, n, n + 1)

    pl.when(jnp.logical_not(has_up))(lambda: no_halo(True))
    pl.when(jnp.logical_not(has_down))(lambda: no_halo(False))

    def all_here():
        both = has_up & has_down
        pl.when(both)(lambda: pl.semaphore_wait(barrier, 8))
        pl.when(jnp.logical_not(both))(lambda: pl.semaphore_wait(barrier, 5))

    zero_rows(v0, 0, 1)
    zero_rows(v0, ROWS + 1, ROWS + 2)
    pack_off[...] = jnp.zeros(pack_off.shape, BF)
    for i in range(1, ROWS + 1):
        v0[i, 192:CPAD, :] = jnp.zeros((CPAD - 192, WIDE), BF)

    lane = lax.broadcasted_iota(jnp.int32, (1, BLK), 1)

    def pack_tiles(tiles, side):
        total = None
        for y, tile in enumerate(tiles):
            shift = 8 * y if side == 0 else 8 * y + 8
            moved = pltpu.roll(tile, shift, 1) if shift else tile
            here = (lane >= 8 * y) & (lane < 8 * y + 8)
            total = jnp.where(here, moved, 0.0 if total is None else total)
        return total

    def unpack(from_right, from_left, y):
        a = pltpu.roll(from_right, (128 - 8 * y) % 128, 1) if y else from_right
        b = pltpu.roll(from_left, 120 - 8 * y, 1)
        return jnp.where(lane < 8, a, jnp.where(lane >= 120, b, 0.0))

    def squeeze(tile):
        total = jnp.zeros((16, BLK), F32)
        for k in range(4):
            moved = pltpu.roll(tile[16 * k:16 * k + 16], 16 * k + 8, 1)
            total = jnp.where((lane >= 16 * k) & (lane < 16 * k + 16), moved, total)
        return total.astype(BF)

    def expand(small, k):
        return pltpu.roll(small.astype(F32), 120 - 16 * k, 1)

    def put_margin(row, small):
        for k in range(4):
            wide = jnp.where((lane < 8) | (lane >= 120), expand(small, k), 0.0)
            row[16 * k:16 * k + 16, COLS:WIDE] = wide.astype(BF)

    def rows_send(kind, up_row, up_dst, down_row, down_dst):
        send(kind, UP, up_row.at[:, 0:COLS], up_dst.at[:, 0:COLS])
        send(kind, DOWN, down_row.at[:, 0:COLS], down_dst.at[:, 0:COLS])
        sq_out[kind, 0] = squeeze(up_row[:, COLS:WIDE].astype(F32))
        sq_out[kind, 1] = squeeze(down_row[:, COLS:WIDE].astype(F32))
        send(kind + KINDS, UP, sq_out.at[kind, 0], sq_in.at[kind, 1])
        send(kind + KINDS, DOWN, sq_out.at[kind, 1], sq_in.at[kind, 0])

    def rows_recv(kind, up_dst, down_dst):
        wait_recv(kind + KINDS, UP, sq_in.at[kind, 0])
        wait_recv(kind + KINDS, DOWN, sq_in.at[kind, 1])
        wait_recv(kind, UP, up_dst.at[:, 0:COLS])
        wait_recv(kind, DOWN, down_dst.at[:, 0:COLS])
        pl.when(has_up)(lambda: put_margin(up_dst, sq_in[kind, 0]))
        pl.when(has_down)(lambda: put_margin(down_dst, sq_in[kind, 1]))

    def rows_sent(kind, up_row, down_row):
        wait_send(kind, UP, up_row.at[:, 0:COLS])
        wait_send(kind, DOWN, down_row.at[:, 0:COLS])
        wait_send(kind + KINDS, UP, sq_out.at[kind, 0])
        wait_send(kind + KINDS, DOWN, sq_out.at[kind, 1])

    load_off[0].wait()
    load_off[1].wait()
    def stage_off(j):
        stage[j] = raw_off[:, j * BLK:(j + 1) * BLK].astype(F32)

    stage_off(0)
    stage_off(NB - 1)

    def staged(channels, y, j):
        return stage[j, pl.ds(y, channels, stride=ROWS), :]

    pack_off[0, 0:CIN, :] = pack_tiles(
        [staged(CIN, y, 0) for y in range(ROWS)], 0).astype(BF)
    pack_off[1, 0:CIN, :] = pack_tiles(
        [staged(CIN, y, NB - 1) for y in range(ROWS)], 1).astype(BF)
    all_here()
    send(S_OFF, LEFT, pack_off.at[0], got_off.at[0])
    send(S_OFF, RIGHT, pack_off.at[1], got_off.at[1])

    for y in (2, 3, 4, 5, 0, 1, 6, 7):
        hat_load(y).start()

    load_src.wait()
    for j in range(NB):
        stage2[j] = raw_src[:, j * BLK:(j + 1) * BLK].astype(F32)

    def win_row(y, _):
        for k in range(4):
            for j in range(NB):
                near[y, j + 2, k * 16:(k + 1) * 16, :] = stage2[
                    j, pl.ds(k * ROWS + y, 16, stride=4 * ROWS), :].astype(BF)
        return 0

    lax.fori_loop(0, ROWS, win_row, 0)

    def by_reach(row_tile, fn):
        outer = (row_tile < n_lat // 4) | (row_tile >= n_lat - n_lat // 4)
        pl.when(outer)(lambda: fn(2))
        pl.when(jnp.logical_not(outer))(lambda: fn(1))

    def to_left(rows, n, buf=win):
        return buf.at[rows, 2:2 + n]

    def to_right(rows, n, buf=win):
        return buf.at[rows, 6 - n:6]

    def from_left(rows, n, buf=win):
        return buf.at[rows, 2 - n:2]

    def from_right(rows, n, buf=win):
        return buf.at[rows, 6:6 + n]

    INNER, TOP, BOTTOM = slice(0, 8), slice(0, 2), slice(10, 12)
    FIRST, LAST = slice(0, 2), slice(6, 8)
    odd = lax.rem(lon, 2) == 1
    even = jnp.logical_not(odd)

    def source_columns(n):
        send(S_SRC, LEFT, to_left(INNER, n, near), from_right(INNER, n, near))
        send(S_SRC, RIGHT, to_right(INNER, n, near), from_left(INNER, n, near))

    def source_columns_in(n):
        wait_recv(S_SRC, RIGHT, from_right(INNER, n, near))
        wait_recv(S_SRC, LEFT, from_left(INNER, n, near))

    def source_columns_sent(n):
        wait_send(S_SRC, LEFT, to_left(INNER, n, near))
        wait_send(S_SRC, RIGHT, to_right(INNER, n, near))

    def source_rows():
        send(S_SRC, UP, near.at[FIRST, 2:6], win.at[BOTTOM, 2:6])
        send(S_SRC, DOWN, near.at[LAST, 2:6], win.at[TOP, 2:6])

        @pl.when(even)
        def _():
            by_reach(lat - 1, lambda n: send(S_SRC, UL, to_left(FIRST, n, near), from_right(BOTTOM, n)))
            by_reach(lat + 1, lambda n: send(S_SRC, DL, to_left(LAST, n, near), from_right(TOP, n)))

        @pl.when(odd)
        def _():
            by_reach(lat - 1, lambda n: send(S_SRC, UR, to_right(FIRST, n, near), from_left(BOTTOM, n)))
            by_reach(lat + 1, lambda n: send(S_SRC, DR, to_right(LAST, n, near), from_left(TOP, n)))

    def source_rows_sent():
        wait_send(S_SRC, UP, near.at[FIRST, 2:6])
        wait_send(S_SRC, DOWN, near.at[LAST, 2:6])

        @pl.when(even)
        def _():
            by_reach(lat - 1, lambda n: wait_send(S_SRC, UL, to_left(FIRST, n, near)))
            by_reach(lat + 1, lambda n: wait_send(S_SRC, DL, to_left(LAST, n, near)))

        @pl.when(odd)
        def _():
            by_reach(lat - 1, lambda n: wait_send(S_SRC, UR, to_right(FIRST, n, near)))
            by_reach(lat + 1, lambda n: wait_send(S_SRC, DR, to_right(LAST, n, near)))

    def relay(kind, rows, n):
        pl.when(even)(lambda: send(kind, RIGHT, to_right(rows, n), from_left(rows, n)))
        pl.when(odd)(lambda: send(kind, LEFT, to_left(rows, n), from_right(rows, n)))

    def relay_in(kind, rows, n):
        pl.when(even)(lambda: wait_recv(kind, RIGHT, from_right(rows, n)))
        pl.when(odd)(lambda: wait_recv(kind, LEFT, from_left(rows, n)))

    def relay_sent(kind, rows, n):
        pl.when(even)(lambda: wait_send(kind, RIGHT, to_right(rows, n)))
        pl.when(odd)(lambda: wait_send(kind, LEFT, to_left(rows, n)))

    def each_relay(fn):
        pl.when(has_up)(lambda: by_reach(lat, lambda n: fn(S_SRC_LO, TOP, n)))
        pl.when(has_down)(lambda: by_reach(lat, lambda n: fn(S_SRC_HI, BOTTOM, n)))

    def source_rows_in():
        wait_recv(S_SRC, UP, win.at[TOP, 2:6])
        wait_recv(S_SRC, DOWN, win.at[BOTTOM, 2:6])
        each_relay(relay)

    def source_corners_in():
        @pl.when(odd)
        def _():
            by_reach(lat, lambda n: wait_recv(S_SRC, UR, from_right(TOP, n)))
            by_reach(lat, lambda n: wait_recv(S_SRC, DR, from_right(BOTTOM, n)))

        @pl.when(even)
        def _():
            by_reach(lat, lambda n: wait_recv(S_SRC, UL, from_left(TOP, n)))
            by_reach(lat, lambda n: wait_recv(S_SRC, DL, from_left(BOTTOM, n)))

        each_relay(relay_in)

    by_reach(lat, source_columns)

    load_off[2].wait()
    for j in range(1, NB - 1):
        stage_off(j)

    def v0_row(y, _):
        for j in range(NB):
            v0[y + 1, 0:CIN, j * BLK:(j + 1) * BLK] = staged(CIN, y, j).astype(BF)
        return 0

    lax.fori_loop(0, ROWS, v0_row, 0)

    load_cur.wait()
    for j in range(NB):
        stage2[j] = raw_cur[:, j * BLK:(j + 1) * BLK].astype(F32)

    def cur_staged(y, j):
        return stage2[j, pl.ds(y, 64, stride=ROWS), :]

    def cur_row(y, _):
        for j in range(NB):
            joined[y + 1, 0:64, j * BLK:(j + 1) * BLK] = cur_staged(y, j).astype(BF)
        return 0

    lax.fori_loop(0, ROWS, cur_row, 0)
    pack_cur[0] = pack_tiles([cur_staged(y, 0) for y in range(ROWS)], 0).astype(BF)
    pack_cur[1] = pack_tiles([cur_staged(y, NB - 1) for y in range(ROWS)], 1).astype(BF)

    send(S_CURM, LEFT, pack_cur.at[0], got_cur.at[0])
    send(S_CURM, RIGHT, pack_cur.at[1], got_cur.at[1])

    for load in load_weights:
        load.wait()
    w1[...] = jnp.zeros(w1.shape, BF)
    for a in range(3):
        for b in range(3):
            w1[b * 64:(b + 1) * 64, a * CPAD:a * CPAD + CIN] = w1_ref[3 * a + b]
            wg[b * 64:(b + 1) * 64, a * 128:(a + 1) * 128] = wg_ref[3 * a + b]
    for b in range(3):
        w2[b * 64:(b + 1) * 64, :] = jnp.concatenate([w2_ref[3 * a + b] for a in range(3)], axis=1)
        for r in range(4):
            wr[r, b * 64:(b + 1) * 64, :] = jnp.concatenate(
                [wr_ref[r, 3 * a + b] for a in range(3)], axis=1)
    wm[...] = wm_ref[...].reshape(TAPS * 64, 144).astype(F32).T.astype(BF)
    row_id = lax.broadcasted_iota(jnp.int32, (64, 64), 0)
    col_id = lax.broadcasted_iota(jnp.int32, (64, 64), 1)
    perm = (row_id == (col_id % 16) * 4 + col_id // 16).astype(BF)
    wd[...] = jnp.concatenate(
        [jnp.dot(wd_ref[t], perm, preferred_element_type=F32).astype(BF) for t in range(TAPS)], axis=1)

    def spread(p):
        n = p.shape[1]
        return pltpu.roll(p[0:64], 1, 1) + p[64:128] + pltpu.roll(p[128:192], n - 1, 1)

    def conv_row(src, i, weight):
        x = src[pl.ds(i, 3)].reshape(3 * src.shape[1], WIDE)
        return spread(jnp.dot(weight, x, preferred_element_type=F32))

    def row_out(kind, buf, m, n):
        rows_send(kind, buf.at[m + n], buf.at[ROWS + m + n],
                  buf.at[ROWS + m - 1 - n], buf.at[m - 1 - n])

    def row_in(kind, buf, m, n):
        rows_recv(kind, buf.at[m - 1 - n], buf.at[ROWS + m + n])

    def row_sent(kind, buf, m, n):
        rows_sent(kind, buf.at[m + n], buf.at[ROWS + m - 1 - n])

    def rows_loop(lo, hi, fn):
        lax.fori_loop(lo, hi, fn, 0, unroll=True)

    def edge4(fn):
        return lambda i, c: fn(i + (i // 2) * (ROWS - 4), c)

    def ring4(fn):
        return lambda i, c: fn(i - 1 + (i // 2) * (ROWS - 2), c)

    wait_recv(S_OFF, RIGHT, got_off.at[0])
    wait_recv(S_OFF, LEFT, got_off.at[1])
    def v0_margin(y):
        v0[y + 1, 0:CIN, COLS:WIDE] = unpack(
            got_off[0, 0:CIN, :].astype(F32), got_off[1, 0:CIN, :].astype(F32), y).astype(BF)

    v0_margin(0)
    v0_margin(ROWS - 1)
    part_out[0] = spread(jnp.dot(w1[:, 2 * CPAD:], v0[1], preferred_element_type=F32)).astype(BF)
    part_out[1] = spread(jnp.dot(w1[:, :CPAD], v0[ROWS], preferred_element_type=F32)).astype(BF)
    rows_send(S_PART, part_out.at[0], part_in.at[1], part_out.at[1], part_in.at[0])
    source_rows()
    for y in range(1, ROWS - 1):
        v0_margin(y)

    def h1_row(y, _):
        h1[y + 2] = leaky(conv_row(v0, y, w1[...])).astype(BF)
        return 0

    h1_row(1, 0)
    h1_row(ROWS - 2, 0)
    row_out(S_H1_IN, h1, 2, 1)
    rows_loop(2, ROWS - 2, h1_row)
    part_own[0] = conv_row(v0, 0, w1[...])
    part_own[1] = conv_row(v0, ROWS - 1, w1[...])

    total = NB * n_lon
    shift = total.bit_length() - 1
    col_base = lon * NB - 2

    def sample_row(y, src, first, count):
        for j in range(NB):
            for t in range(TAPS):
                parts = []
                for f in range(2):
                    ix = foot_ref[y, j, f, t]
                    row = jnp.clip(lax.shift_right_logical(ix, shift) - first, 0, count - 1)
                    col = jnp.minimum(lax.bitwise_and(ix - col_base, total - 1), WIN_COLS - 1)
                    parts.append((src[row, col].astype(F32) * scale_ref[y, j, f, t]).astype(BF))
                tile = hats[y, (j * K2 + 2 * t) * BLK:(j * K2 + 2 * t + 2) * BLK, :]
                sampled[y, t * 64:(t + 1) * 64, j * BLK:(j + 1) * BLK] = jnp.dot(
                    jnp.concatenate(parts, axis=1), tile, preferred_element_type=F32)
        return 0

    by_reach(lat, source_columns_in)
    for y in range(2, ROWS - 2):
        hat_load(y).wait()
    rows_loop(2, ROWS - 2, lambda y, _: sample_row(y, near, lat * ROWS, ROWS))
    win[2:2 + ROWS] = near[...]

    rows_recv(S_PART, part_in.at[0], part_in.at[1])
    h1[2] = leaky(part_own[0] + part_in[0].astype(F32)).astype(BF)
    h1[ROWS + 1] = leaky(part_own[1] + part_in[1].astype(F32)).astype(BF)

    row_out(S_H1, h1, 2, 0)

    def in_frame(y):
        g = lat * ROWS + y
        return (g >= 0) & (g < n_lat * ROWS)

    def h2_row(y, _):
        v = leaky(conv_row(h1, y + 1, w2[...]))
        v = jnp.where(in_frame(y), v, 0.0)
        h2[y + 1, 0:64] = pltpu.roll(v, 1, 1).astype(BF)
        h2[y + 1, 64:128] = v.astype(BF)
        h2[y + 1, 128:192] = pltpu.roll(v, WIDE - 1, 1).astype(BF)
        return 0

    rows_loop(1, ROWS - 1, h2_row)

    source_rows_in()
    source_corners_in()
    for y in (0, 1, ROWS - 2, ROWS - 1):
        hat_load(y).wait()
    rows_loop(0, 4, edge4(lambda y, _: sample_row(y, win, lat * ROWS - 2, WIN_ROWS)))

    def aligned_row(y, _):
        x = h2[pl.ds(y, 3)].reshape(576, WIDE)[:, 0:COLS]
        logits = jnp.dot(wm[...], x, preferred_element_type=F32)
        mod = 1.0 / (1.0 + jnp.exp(-logits))
        for t in range(TAPS):
            m = mod[t * 16:(t + 1) * 16]
            for k in range(4):
                lo = t * 64 + k * 16
                modulated[lo:lo + 16, :] = (m * sampled[y, lo:lo + 16, :]).astype(BF)
        joined[y + 1, 64:128, 0:COLS] = jnp.dot(
            wd[...], modulated[...], preferred_element_type=F32).astype(BF)
        return 0

    rows_loop(2, ROWS - 2, aligned_row)

    wait_recv(S_CURM, RIGHT, got_cur.at[0])
    wait_recv(S_CURM, LEFT, got_cur.at[1])
    for y in range(ROWS):
        joined[y + 1, 0:64, COLS:WIDE] = unpack(
            got_cur[0].astype(F32), got_cur[1].astype(F32), y).astype(BF)
    row_in(S_H1_IN, h1, 2, 1)
    row_in(S_H1, h1, 2, 0)
    rows_send(S_CUR, joined.at[1, 0:64], joined.at[ROWS + 1, 0:64],
              joined.at[ROWS, 0:64], joined.at[0, 0:64])
    rows_loop(0, 4, ring4(h2_row))
    aligned_row(0, 0)
    aligned_row(ROWS - 1, 0)

    send(S_AL, UP, joined.at[1, 64:128, 0:COLS], joined.at[ROWS + 1, 64:128, 0:COLS])
    send(S_AL, DOWN, joined.at[ROWS, 64:128, 0:COLS], joined.at[0, 64:128, 0:COLS])
    aligned_row(1, 0)
    aligned_row(ROWS - 2, 0)
    def corner_tile(i):
        first = joined[i, 64:128, 0:BLK].astype(F32)
        last = joined[i, 64:128, COLS - BLK:COLS].astype(F32)
        return squeeze(jnp.where(lane < 64, first, last))

    sq_out[S_ALM, 0] = corner_tile(1)
    sq_out[S_ALM, 1] = corner_tile(ROWS)
    for side, d in AL_CORNERS:
        send(S_ALM, d, sq_out.at[S_ALM, side], got_corner.at[OPP[d]])
    pack_al[0] = pack_tiles(
        [joined[y + 1, 64:128, 0:BLK].astype(F32) for y in range(ROWS)], 0).astype(BF)
    pack_al[1] = pack_tiles(
        [joined[y + 1, 64:128, COLS - BLK:COLS].astype(F32) for y in range(ROWS)], 1).astype(BF)
    send(S_ALM, LEFT, pack_al.at[0], got_al.at[0])
    send(S_ALM, RIGHT, pack_al.at[1], got_al.at[1])
    wait_recv(S_ALM, RIGHT, got_al.at[0])
    wait_recv(S_ALM, LEFT, got_al.at[1])
    for y in range(ROWS):
        joined[y + 1, 64:128, COLS:WIDE] = unpack(
            got_al[0].astype(F32), got_al[1].astype(F32), y).astype(BF)

    def corners_in():
        for _, d in AL_CORNERS:
            wait_recv(S_ALM, d, got_corner.at[d])

        def put(i, from_right, from_left):
            for k in range(4):
                a, b = expand(got_corner[from_right], k), expand(got_corner[from_left], k)
                wide = jnp.where(lane < 8, a, jnp.where(lane >= 120, b, 0.0))
                joined[i, 64 + 16 * k:80 + 16 * k, COLS:WIDE] = wide.astype(BF)

        pl.when(has_up)(lambda: put(0, UR, UL))
        pl.when(has_down)(lambda: put(ROWS + 1, DR, DL))

    def t0_row(y, _):
        t0[y + 2] = leaky(conv_row(joined, y, wg[...])).astype(BF)
        return 0

    def inner_row(dst, src, r):
        def go(y, _):
            v = jnp.maximum(conv_row(src, y + 1, wr[r]), 0.0)
            dst[y + 1] = jnp.where(in_frame(y), v, 0.0).astype(BF)
            return 0
        return go

    def t1_row(y, _):
        t1[y + 2] = (t0[y + 2].astype(F32) + conv_row(i0, y, wr[1])).astype(BF)
        return 0

    def out_copy(y):
        return pltpu.make_async_copy(out_ref.at[y], out_hbm.at[y], out_sem.at[y])

    def final_row(y, _):
        trunk = (t1[y + 2].astype(F32) + conv_row(i1, y, wr[3])).astype(BF)
        trunk = trunk[:, 0:COLS].astype(F32)
        out_ref[y] = (trunk + joined[y + 1, 64:128, 0:COLS].astype(F32)).astype(BF)
        out_copy(y).start()
        return 0

    t0_row(1, 0)
    t0_row(ROWS - 2, 0)
    row_out(S_T0_IN, t0, 2, 1)
    rows_loop(2, ROWS - 2, t0_row)
    rows_recv(S_CUR, joined.at[0, 0:64], joined.at[ROWS + 1, 0:64])
    corners_in()
    wait_recv(S_AL, UP, joined.at[0, 64:128, 0:COLS])
    wait_recv(S_AL, DOWN, joined.at[ROWS + 1, 64:128, 0:COLS])
    t0_row(0, 0)
    t0_row(ROWS - 1, 0)
    row_out(S_T0, t0, 2, 0)
    inner0 = inner_row(i0, t0, 0)
    inner1 = inner_row(i1, t1, 2)
    rows_loop(1, ROWS - 1, inner0)
    rows_loop(2, ROWS - 2, t1_row)
    row_in(S_T0_IN, t0, 2, 1)
    row_in(S_T0, t0, 2, 0)
    rows_loop(0, 4, ring4(inner0))
    t1_row(0, 0)
    t1_row(ROWS - 1, 0)
    row_out(S_T1, t1, 2, 0)
    t1_row(1, 0)
    t1_row(ROWS - 2, 0)
    row_out(S_T1_IN, t1, 2, 1)
    rows_loop(1, ROWS - 1, inner1)
    rows_loop(2, ROWS - 2, final_row)
    row_in(S_T1, t1, 2, 0)
    inner1(0, 0)
    inner1(ROWS - 1, 0)
    final_row(1, 0)
    final_row(ROWS - 2, 0)
    row_in(S_T1_IN, t1, 2, 1)
    inner1(-1, 0)
    inner1(ROWS, 0)
    final_row(0, 0)
    final_row(ROWS - 1, 0)

    for y in range(ROWS):
        out_copy(y).wait()
    wait_send(S_OFF, LEFT, pack_off.at[0])
    wait_send(S_OFF, RIGHT, pack_off.at[1])
    by_reach(lat, source_columns_sent)
    source_rows_sent()
    each_relay(relay_sent)
    rows_sent(S_PART, part_out.at[0], part_out.at[1])
    for side, d in AL_CORNERS:
        wait_send(S_ALM, d, sq_out.at[S_ALM, side])
    wait_send(S_ALM, LEFT, pack_al.at[0])
    wait_send(S_ALM, RIGHT, pack_al.at[1])
    wait_send(S_CURM, LEFT, pack_cur.at[0])
    wait_send(S_CURM, RIGHT, pack_cur.at[1])
    rows_sent(S_CUR, joined.at[1, 0:64], joined.at[ROWS, 0:64])
    wait_send(S_AL, UP, joined.at[1, 64:128, 0:COLS])
    wait_send(S_AL, DOWN, joined.at[ROWS, 64:128, 0:COLS])
    for kind, buf in ((S_H1, h1), (S_T0, t0), (S_T1, t1)):
        row_sent(kind, buf, 2, 0)
        row_sent(kind + 1, buf, 2, 1)


def shards(
    offset_input, current, source, first_weight, second_weight, mask_weight, deform_weight,
    merge_weight, residual_weight, footprint, tile_scale, hats,
):
    n_lon, n_lat = lax.axis_size("lon"), lax.axis_size("lat")
    assert n_lon & (n_lon - 1) == 0
    hbm = pl.BlockSpec(memory_space=pl.ANY)
    V = pltpu.VMEM
    out = pl.pallas_call(
        functools.partial(kernel, n_lon, n_lat),
        out_shape=jax.ShapeDtypeStruct((ROWS, 64, COLS), BF),
        in_specs=[hbm] * 12,
        out_specs=hbm,
        scratch_shapes=[
            pltpu.SMEM((ROWS, NB, 2, TAPS), jnp.int32), pltpu.SMEM((ROWS, NB, 2, TAPS), F32),
            V((ROWS, 64, COLS), BF),
            V((9, 64, CIN), BF), V((9, 64, 64), BF), V((9, 64, 144), BF), V((9, 64, 64), BF),
            V((9, 64, 128), BF), V((4, 9, 64, 64), BF),
            V((CIN * ROWS, COLS), BF), V((64 * ROWS, COLS), BF), V((64 * ROWS, COLS), BF),
            V((NB, CIN * ROWS, BLK), F32),
            V((NB, 64 * ROWS, BLK), F32),
            V((ROWS, NB * K2 * BLK, BLK), BF),
            V((ROWS, WIN_COLS, 64, BLK), BF),
            V((WIN_ROWS, WIN_COLS, 64, BLK), BF),
            V((ROWS, TAPS * 64, COLS), F32),
            V((TAPS * 64, COLS), BF),
            V((ROWS + 2, CPAD, WIDE), BF),
            V((ROWS + 4, 64, WIDE), BF),
            V((ROWS + 2, 192, WIDE), BF),
            V((ROWS + 2, 128, WIDE), BF),
            V((ROWS + 4, 64, WIDE), BF),
            V((ROWS + 2, 64, WIDE), BF),
            V((ROWS + 4, 64, WIDE), BF),
            V((ROWS + 2, 64, WIDE), BF),
            V((192, 3 * CPAD), BF), V((192, 192), BF), V((144, 576), BF), V((64, 576), BF),
            V((192, 384), BF), V((4, 192, 192), BF),
            V((2, 208, BLK), BF), V((2, 208, BLK), BF),
            V((2, 64, BLK), BF), V((2, 64, BLK), BF),
            V((2, 64, BLK), BF), V((2, 64, BLK), BF), V((8, 16, BLK), BF),
            V((2, 64, WIDE), BF), V((2, 64, WIDE), BF), V((2, 64, WIDE), F32),
            V((KINDS, 2, 16, BLK), BF), V((KINDS, 2, 16, BLK), BF),
            pltpu.SemaphoreType.DMA((13,)),
            pltpu.SemaphoreType.DMA((ROWS,)),
            pltpu.SemaphoreType.DMA((ROWS,)),
            pltpu.SemaphoreType.DMA((2 * KINDS, 8)),
            pltpu.SemaphoreType.DMA((2 * KINDS, 8)),
        ],
        compiler_params=pltpu.CompilerParams(
            collective_id=0, has_side_effects=True, vmem_limit_bytes=60 * 2**20),
    )(
        offset_input.reshape(CIN * ROWS, COLS),
        current.reshape(64 * ROWS, COLS),
        source.reshape(64 * ROWS, COLS),
        first_weight, second_weight, mask_weight.transpose(0, 2, 1), deform_weight, merge_weight,
        residual_weight.reshape(4, 9, 64, 64),
        footprint.transpose(0, 1, 3, 2), tile_scale.transpose(0, 1, 3, 2),
        hats.reshape(ROWS, NB * K2 * BLK, BLK),
    )
    return out.transpose(1, 0, 2)


def solution(mesh):
    in_specs = (
        P(None, "lat", "lon"),
        P(None, "lat", "lon"),
        P(None, "lat", "lon"),
        P(),
        P(),
        P(),
        P(),
        P(),
        P(),
        P("lat", "lon", None, None),
        P("lat", "lon", None, None),
        P("lat", "lon", None, None, None, None),
    )
    return jax.shard_map(
        shards, mesh=mesh, in_specs=in_specs, out_specs=P(None, "lat", "lon"), check_vma=False)
```

```python
import functools

import jax
import jax.numpy as jnp
from jax import lax
from jax.experimental import pallas as pl
from jax.experimental.pallas import tpu as pltpu
from jax.sharding import PartitionSpec as P

BF = jnp.bfloat16
F32 = jnp.float32
MESH = pl.DeviceIdType.MESH

BLK = 128
ROWS = 8
COLS = 512
WIDE = 640
CIN = 196
CPAD = 256
NB = COLS // BLK
WIN_ROWS = ROWS + 4
WIN_COLS = NB + 4
TAPS = 9
K2 = 18

LEFT, RIGHT, UP, DOWN, UL, UR, DL, DR = range(8)
AL_CORNERS = ((0, UL), (0, UR), (1, DL), (1, DR))
OPP = (RIGHT, LEFT, DOWN, UP, DR, DL, UR, UL)
(S_OFF, S_SRC, S_SRC_LO, S_SRC_HI, S_CURM, S_CUR, S_PART, S_H1, S_H1_IN, S_ALM, S_AL,
 S_T0, S_T0_IN, S_T1, S_T1_IN) = range(15)
KINDS = 15


def leaky(v):
    return jnp.where(v > 0, v, 0.1 * v)


def kernel(
    n_lon, n_lat,
    off_hbm, cur_hbm, src_hbm, w1_hbm, w2_hbm, wm_hbm, wd_hbm, wg_hbm, wr_hbm,
    foot_hbm, scale_hbm, hats_hbm, out_hbm,
    foot_ref, scale_ref, out_ref,
    w1_ref, w2_ref, wm_ref, wd_ref, wg_ref, wr_ref,
    raw_off, raw_src, raw_cur, stage, stage2, hats, near, win, sampled, modulated,
    v0, h1, h2, joined, t0, i0, t1, i1,
    w1, w2, wm, wd, wg, wr,
    pack_off, got_off, pack_cur, got_cur, pack_al, got_al, got_corner,
    part_out, part_in, part_own, sq_out, sq_in,
    load_sem, hat_sem, out_sem, send_sem, recv_sem,
):
    lon = lax.axis_index("lon")
    lat = lax.axis_index("lat")
    left = lax.rem(lon + n_lon - 1, n_lon)
    right = lax.rem(lon + 1, n_lon)
    has_up = lat > 0
    has_down = lat < n_lat - 1
    nb = {
        LEFT: (None, (left, lat)), RIGHT: (None, (right, lat)),
        UP: (has_up, (lon, lat - 1)), DOWN: (has_down, (lon, lat + 1)),
        UL: (has_up, (left, lat - 1)), UR: (has_up, (right, lat - 1)),
        DL: (has_down, (left, lat + 1)), DR: (has_down, (right, lat + 1)),
    }

    def guarded(cond, fn):
        if cond is None:
            fn()
        else:
            pl.when(cond)(fn)

    def copy(kind, direction, src, dst):
        return pltpu.make_async_remote_copy(
            src_ref=src, dst_ref=dst,
            send_sem=send_sem.at[kind, direction],
            recv_sem=recv_sem.at[kind, OPP[direction]],
            device_id=nb[direction][1], device_id_type=MESH,
        )

    def send(kind, direction, src, dst):
        guarded(nb[direction][0], lambda: copy(kind, direction, src, dst).start())

    def wait_send(kind, direction, src):
        def go():
            pltpu.make_async_remote_copy(
                src_ref=src, dst_ref=src, send_sem=send_sem.at[kind, direction],
                recv_sem=recv_sem.at[kind, direction],
                device_id=nb[direction][1], device_id_type=MESH,
            ).wait_send()
        guarded(nb[direction][0], go)

    def wait_recv(kind, direction, dst):
        def go():
            pltpu.make_async_remote_copy(
                src_ref=dst, dst_ref=dst, send_sem=send_sem.at[kind, direction],
                recv_sem=recv_sem.at[kind, direction],
                device_id=nb[direction][1], device_id_type=MESH,
            ).wait_recv()
        guarded(nb[direction][0], go)

    barrier = pltpu.get_barrier_semaphore()
    for d in range(8):
        guarded(nb[d][0], lambda d=d: pl.semaphore_signal(
            barrier, inc=1, device_id=nb[d][1], device_id_type=MESH))

    def off_load(lo, hi, n):
        return pltpu.make_async_copy(off_hbm.at[:, lo:hi], raw_off.at[:, lo:hi], load_sem.at[n])

    load_off = [off_load(0, BLK, 0), off_load(COLS - BLK, COLS, 11), off_load(BLK, COLS - BLK, 12)]
    load_src = pltpu.make_async_copy(src_hbm, raw_src, load_sem.at[1])
    load_cur = pltpu.make_async_copy(cur_hbm, raw_cur, load_sem.at[2])
    for load in load_off:
        load.start()
    load_src.start()
    load_weights = [
        pltpu.make_async_copy(a, b, load_sem.at[3 + n])
        for n, (a, b) in enumerate((
            (w1_hbm, w1_ref), (w2_hbm, w2_ref), (wm_hbm, wm_ref), (wd_hbm, wd_ref),
            (wg_hbm, wg_ref), (wr_hbm, wr_ref), (foot_hbm, foot_ref), (scale_hbm, scale_ref)))
    ]
    for load in load_weights:
        load.start()
    load_cur.start()

    def hat_load(y):
        return pltpu.make_async_copy(hats_hbm.at[y], hats.at[y], hat_sem.at[y])

    def zero_rows(buf, lo, hi):
        buf[lo:hi] = jnp.zeros((hi - lo,) + buf.shape[1:], buf.dtype)

    def no_halo(top):
        for buf, m in ((h1, 2), (joined, 1), (t0, 2), (t1, 2)):
            if top:
                zero_rows(buf, 0, m)
            else:
                zero_rows(buf, ROWS + m, ROWS + 2 * m)
        n = 0 if top else 1
        zero_rows(part_in, n, n + 1)

    pl.when(jnp.logical_not(has_up))(lambda: no_halo(True))
    pl.when(jnp.logical_not(has_down))(lambda: no_halo(False))

    def all_here():
        both = has_up & has_down
        pl.when(both)(lambda: pl.semaphore_wait(barrier, 8))
        pl.when(jnp.logical_not(both))(lambda: pl.semaphore_wait(barrier, 5))

    zero_rows(v0, 0, 1)
    zero_rows(v0, ROWS + 1, ROWS + 2)
    pack_off[...] = jnp.zeros(pack_off.shape, BF)
    for i in range(1, ROWS + 1):
        v0[i, 192:CPAD, :] = jnp.zeros((CPAD - 192, WIDE), BF)

    lane = lax.broadcasted_iota(jnp.int32, (1, BLK), 1)

    def pack_tiles(tiles, side):
        total = None
        for y, tile in enumerate(tiles):
            shift = 8 * y if side == 0 else 8 * y + 8
            moved = pltpu.roll(tile, shift, 1) if shift else tile
            here = (lane >= 8 * y) & (lane < 8 * y + 8)
            total = jnp.where(here, moved, 0.0 if total is None else total)
        return total

    def unpack(from_right, from_left, y):
        a = pltpu.roll(from_right, (128 - 8 * y) % 128, 1) if y else from_right
        b = pltpu.roll(from_left, 120 - 8 * y, 1)
        return jnp.where(lane < 8, a, jnp.where(lane >= 120, b, 0.0))

    def squeeze(tile):
        total = jnp.zeros((16, BLK), F32)
        for k in range(4):
            moved = pltpu.roll(tile[16 * k:16 * k + 16], 16 * k + 8, 1)
            total = jnp.where((lane >= 16 * k) & (lane < 16 * k + 16), moved, total)
        return total.astype(BF)

    def expand(small, k):
        return pltpu.roll(small.astype(F32), 120 - 16 * k, 1)

    def put_margin(row, small, there):
        for k in range(4):
            wide = jnp.where(((lane < 8) | (lane >= 120)) & there, expand(small, k), 0.0)
            row[16 * k:16 * k + 16, COLS:WIDE] = wide.astype(BF)

    def rows_send(kind, up_row, up_dst, down_row, down_dst):
        send(kind, UP, up_row.at[:, 0:COLS], up_dst.at[:, 0:COLS])
        send(kind, DOWN, down_row.at[:, 0:COLS], down_dst.at[:, 0:COLS])
        sq_out[kind, 0] = squeeze(up_row[:, COLS:WIDE].astype(F32))
        sq_out[kind, 1] = squeeze(down_row[:, COLS:WIDE].astype(F32))
        send(kind + KINDS, UP, sq_out.at[kind, 0], sq_in.at[kind, 1])
        send(kind + KINDS, DOWN, sq_out.at[kind, 1], sq_in.at[kind, 0])

    def rows_recv(kind, up_dst, down_dst):
        wait_recv(kind + KINDS, UP, sq_in.at[kind, 0])
        wait_recv(kind + KINDS, DOWN, sq_in.at[kind, 1])
        wait_recv(kind, UP, up_dst.at[:, 0:COLS])
        wait_recv(kind, DOWN, down_dst.at[:, 0:COLS])
        put_margin(up_dst, sq_in[kind, 0], has_up)
        put_margin(down_dst, sq_in[kind, 1], has_down)

    def rows_sent(kind, up_row, down_row):
        wait_send(kind, UP, up_row.at[:, 0:COLS])
        wait_send(kind, DOWN, down_row.at[:, 0:COLS])
        wait_send(kind + KINDS, UP, sq_out.at[kind, 0])
        wait_send(kind + KINDS, DOWN, sq_out.at[kind, 1])

    load_off[0].wait()
    load_off[1].wait()
    def stage_off(j):
        stage[j] = raw_off[:, j * BLK:(j + 1) * BLK].astype(F32)

    stage_off(0)
    stage_off(NB - 1)

    def staged(channels, y, j):
        return stage[j, pl.ds(y, channels, stride=ROWS), :]

    pack_off[0, 0:CIN, :] = pack_tiles(
        [staged(CIN, y, 0) for y in range(ROWS)], 0).astype(BF)
    pack_off[1, 0:CIN, :] = pack_tiles(
        [staged(CIN, y, NB - 1) for y in range(ROWS)], 1).astype(BF)
    all_here()
    send(S_OFF, LEFT, pack_off.at[0], got_off.at[0])
    send(S_OFF, RIGHT, pack_off.at[1], got_off.at[1])

    for y in (2, 3, 4, 5, 0, 1, 6, 7):
        hat_load(y).start()

    load_src.wait()
    for j in range(NB):
        stage2[j] = raw_src[:, j * BLK:(j + 1) * BLK].astype(F32)

    def win_row(y, _):
        for k in range(4):
            for j in range(NB):
                near[y, j + 2, k * 16:(k + 1) * 16, :] = stage2[
                    j, pl.ds(k * ROWS + y, 16, stride=4 * ROWS), :].astype(BF)
        return 0

    lax.fori_loop(0, ROWS, win_row, 0)

    def by_reach(row_tile, fn):
        outer = (row_tile < n_lat // 4) | (row_tile >= n_lat - n_lat // 4)
        pl.when(outer)(lambda: fn(2))
        pl.when(jnp.logical_not(outer))(lambda: fn(1))

    def to_left(rows, n, buf=win):
        return buf.at[rows, 2:2 + n]

    def to_right(rows, n, buf=win):
        return buf.at[rows, 6 - n:6]

    def from_left(rows, n, buf=win):
        return buf.at[rows, 2 - n:2]

    def from_right(rows, n, buf=win):
        return buf.at[rows, 6:6 + n]

    INNER, TOP, BOTTOM = slice(0, 8), slice(0, 2), slice(10, 12)
    FIRST, LAST = slice(0, 2), slice(6, 8)
    odd = lax.rem(lon, 2) == 1
    even = jnp.logical_not(odd)

    def source_columns(n):
        send(S_SRC, LEFT, to_left(INNER, n, near), from_right(INNER, n, near))
        send(S_SRC, RIGHT, to_right(INNER, n, near), from_left(INNER, n, near))

    def source_columns_in(n):
        wait_recv(S_SRC, RIGHT, from_right(INNER, n, near))
        wait_recv(S_SRC, LEFT, from_left(INNER, n, near))

    def source_columns_sent(n):
        wait_send(S_SRC, LEFT, to_left(INNER, n, near))
        wait_send(S_SRC, RIGHT, to_right(INNER, n, near))

    def source_rows():
        send(S_SRC, UP, near.at[FIRST, 2:6], win.at[BOTTOM, 2:6])
        send(S_SRC, DOWN, near.at[LAST, 2:6], win.at[TOP, 2:6])

        @pl.when(even)
        def _():
            by_reach(lat - 1, lambda n: send(S_SRC, UL, to_left(FIRST, n, near), from_right(BOTTOM, n)))
            by_reach(lat + 1, lambda n: send(S_SRC, DL, to_left(LAST, n, near), from_right(TOP, n)))

        @pl.when(odd)
        def _():
            by_reach(lat - 1, lambda n: send(S_SRC, UR, to_right(FIRST, n, near), from_left(BOTTOM, n)))
            by_reach(lat + 1, lambda n: send(S_SRC, DR, to_right(LAST, n, near), from_left(TOP, n)))

    def source_rows_sent():
        wait_send(S_SRC, UP, near.at[FIRST, 2:6])
        wait_send(S_SRC, DOWN, near.at[LAST, 2:6])

        @pl.when(even)
        def _():
            by_reach(lat - 1, lambda n: wait_send(S_SRC, UL, to_left(FIRST, n, near)))
            by_reach(lat + 1, lambda n: wait_send(S_SRC, DL, to_left(LAST, n, near)))

        @pl.when(odd)
        def _():
            by_reach(lat - 1, lambda n: wait_send(S_SRC, UR, to_right(FIRST, n, near)))
            by_reach(lat + 1, lambda n: wait_send(S_SRC, DR, to_right(LAST, n, near)))

    def relay(kind, rows, n):
        pl.when(even)(lambda: send(kind, RIGHT, to_right(rows, n), from_left(rows, n)))
        pl.when(odd)(lambda: send(kind, LEFT, to_left(rows, n), from_right(rows, n)))

    def relay_in(kind, rows, n):
        pl.when(even)(lambda: wait_recv(kind, RIGHT, from_right(rows, n)))
        pl.when(odd)(lambda: wait_recv(kind, LEFT, from_left(rows, n)))

    def relay_sent(kind, rows, n):
        pl.when(even)(lambda: wait_send(kind, RIGHT, to_right(rows, n)))
        pl.when(odd)(lambda: wait_send(kind, LEFT, to_left(rows, n)))

    def each_relay(fn):
        pl.when(has_up)(lambda: by_reach(lat, lambda n: fn(S_SRC_LO, TOP, n)))
        pl.when(has_down)(lambda: by_reach(lat, lambda n: fn(S_SRC_HI, BOTTOM, n)))

    def source_rows_in():
        wait_recv(S_SRC, UP, win.at[TOP, 2:6])
        wait_recv(S_SRC, DOWN, win.at[BOTTOM, 2:6])
        each_relay(relay)

    def source_corners_in():
        @pl.when(odd)
        def _():
            by_reach(lat, lambda n: wait_recv(S_SRC, UR, from_right(TOP, n)))
            by_reach(lat, lambda n: wait_recv(S_SRC, DR, from_right(BOTTOM, n)))

        @pl.when(even)
        def _():
            by_reach(lat, lambda n: wait_recv(S_SRC, UL, from_left(TOP, n)))
            by_reach(lat, lambda n: wait_recv(S_SRC, DL, from_left(BOTTOM, n)))

        each_relay(relay_in)

    by_reach(lat, source_columns)
    source_rows()

    load_off[2].wait()
    for j in range(1, NB - 1):
        stage_off(j)

    def v0_row(y, _):
        for j in range(NB):
            v0[y + 1, 0:CIN, j * BLK:(j + 1) * BLK] = staged(CIN, y, j).astype(BF)
        return 0

    lax.fori_loop(0, ROWS, v0_row, 0)

    load_cur.wait()
    for j in range(NB):
        stage2[j] = raw_cur[:, j * BLK:(j + 1) * BLK].astype(F32)

    def cur_staged(y, j):
        return stage2[j, pl.ds(y, 64, stride=ROWS), :]

    def cur_row(y, _):
        for j in range(NB):
            joined[y + 1, 0:64, j * BLK:(j + 1) * BLK] = cur_staged(y, j).astype(BF)
        return 0

    lax.fori_loop(0, ROWS, cur_row, 0)
    pack_cur[0] = pack_tiles([cur_staged(y, 0) for y in range(ROWS)], 0).astype(BF)
    pack_cur[1] = pack_tiles([cur_staged(y, NB - 1) for y in range(ROWS)], 1).astype(BF)

    send(S_CURM, LEFT, pack_cur.at[0], got_cur.at[0])
    send(S_CURM, RIGHT, pack_cur.at[1], got_cur.at[1])

    for load in load_weights:
        load.wait()
    w1[...] = jnp.zeros(w1.shape, BF)
    for a in range(3):
        for b in range(3):
            w1[b * 64:(b + 1) * 64, a * CPAD:a * CPAD + CIN] = w1_ref[3 * a + b]
            wg[b * 64:(b + 1) * 64, a * 128:(a + 1) * 128] = wg_ref[3 * a + b]
    for b in range(3):
        w2[b * 64:(b + 1) * 64, :] = jnp.concatenate([w2_ref[3 * a + b] for a in range(3)], axis=1)
        for r in range(4):
            wr[r, b * 64:(b + 1) * 64, :] = jnp.concatenate(
                [wr_ref[r, 3 * a + b] for a in range(3)], axis=1)
    wm[...] = wm_ref[...].reshape(TAPS * 64, 144).astype(F32).T.astype(BF)
    row_id = lax.broadcasted_iota(jnp.int32, (64, 64), 0)
    col_id = lax.broadcasted_iota(jnp.int32, (64, 64), 1)
    perm = (row_id == (col_id % 16) * 4 + col_id // 16).astype(BF)
    wd[...] = jnp.concatenate(
        [jnp.dot(wd_ref[t], perm, preferred_element_type=F32).astype(BF) for t in range(TAPS)], axis=1)

    def spread(p):
        n = p.shape[1]
        return pltpu.roll(p[0:64], 1, 1) + p[64:128] + pltpu.roll(p[128:192], n - 1, 1)

    def conv_row(src, i, weight):
        x = src[pl.ds(i, 3)].reshape(3 * src.shape[1], WIDE)
        return spread(jnp.dot(weight, x, preferred_element_type=F32))

    def row_out(kind, buf, m, n):
        rows_send(kind, buf.at[m + n], buf.at[ROWS + m + n],
                  buf.at[ROWS + m - 1 - n], buf.at[m - 1 - n])

    def row_in(kind, buf, m, n):
        rows_recv(kind, buf.at[m - 1 - n], buf.at[ROWS + m + n])

    def row_sent(kind, buf, m, n):
        rows_sent(kind, buf.at[m + n], buf.at[ROWS + m - 1 - n])

    def rows_loop(lo, hi, fn):
        lax.fori_loop(lo, hi, fn, 0, unroll=True)

    def edge4(fn):
        return lambda i, c: fn(i + (i // 2) * (ROWS - 4), c)

    def ring4(fn):
        return lambda i, c: fn(i - 1 + (i // 2) * (ROWS - 2), c)

    wait_recv(S_OFF, RIGHT, got_off.at[0])
    wait_recv(S_OFF, LEFT, got_off.at[1])
    def v0_margin(y):
        v0[y + 1, 0:CIN, COLS:WIDE] = unpack(
            got_off[0, 0:CIN, :].astype(F32), got_off[1, 0:CIN, :].astype(F32), y).astype(BF)

    v0_margin(0)
    v0_margin(ROWS - 1)
    part_out[0] = spread(jnp.dot(w1[:, 2 * CPAD:], v0[1], preferred_element_type=F32)).astype(BF)
    part_out[1] = spread(jnp.dot(w1[:, :CPAD], v0[ROWS], preferred_element_type=F32)).astype(BF)
    rows_send(S_PART, part_out.at[0], part_in.at[1], part_out.at[1], part_in.at[0])
    for y in range(1, ROWS - 1):
        v0_margin(y)

    def h1_row(y, _):
        h1[y + 2] = leaky(conv_row(v0, y, w1[...])).astype(BF)
        return 0

    h1_row(1, 0)
    h1_row(ROWS - 2, 0)
    row_out(S_H1_IN, h1, 2, 1)
    rows_loop(2, ROWS - 2, h1_row)
    part_own[0] = conv_row(v0, 0, w1[...])
    part_own[1] = conv_row(v0, ROWS - 1, w1[...])

    total = NB * n_lon
    shift = total.bit_length() - 1
    col_base = lon * NB - 2

    def sample_row(y, src, first, count):
        for j in range(NB):
            for t in range(TAPS):
                parts = []
                for f in range(2):
                    ix = foot_ref[y, j, f, t]
                    row = jnp.clip(lax.shift_right_logical(ix, shift) - first, 0, count - 1)
                    col = jnp.minimum(lax.bitwise_and(ix - col_base, total - 1), WIN_COLS - 1)
                    parts.append((src[row, col].astype(F32) * scale_ref[y, j, f, t]).astype(BF))
                tile = hats[y, (j * K2 + 2 * t) * BLK:(j * K2 + 2 * t + 2) * BLK, :]
                sampled[y, t * 64:(t + 1) * 64, j * BLK:(j + 1) * BLK] = jnp.dot(
                    jnp.concatenate(parts, axis=1), tile, preferred_element_type=F32)
        return 0

    by_reach(lat, source_columns_in)
    for y in range(2, ROWS - 2):
        hat_load(y).wait()
    rows_loop(2, ROWS - 2, lambda y, _: sample_row(y, near, lat * ROWS, ROWS))
    win[2:2 + ROWS] = near[...]
    source_rows_in()

    rows_recv(S_PART, part_in.at[0], part_in.at[1])
    h1[2] = leaky(part_own[0] + part_in[0].astype(F32)).astype(BF)
    h1[ROWS + 1] = leaky(part_own[1] + part_in[1].astype(F32)).astype(BF)

    row_out(S_H1, h1, 2, 0)

    def in_frame(y):
        g = lat * ROWS + y
        return (g >= 0) & (g < n_lat * ROWS)

    def h2_row(y, _):
        v = leaky(conv_row(h1, y + 1, w2[...]))
        v = jnp.where(in_frame(y), v, 0.0)
        h2[y + 1, 0:64] = pltpu.roll(v, 1, 1).astype(BF)
        h2[y + 1, 64:128] = v.astype(BF)
        h2[y + 1, 128:192] = pltpu.roll(v, WIDE - 1, 1).astype(BF)
        return 0

    rows_loop(1, ROWS - 1, h2_row)

    source_corners_in()
    for y in (0, 1, ROWS - 2, ROWS - 1):
        hat_load(y).wait()
    rows_loop(0, 4, edge4(lambda y, _: sample_row(y, win, lat * ROWS - 2, WIN_ROWS)))

    def aligned_row(y, _):
        x = h2[pl.ds(y, 3)].reshape(576, WIDE)[:, 0:COLS]
        logits = jnp.dot(wm[...], x, preferred_element_type=F32)
        mod = 1.0 / (1.0 + jnp.exp(-logits))
        for t in range(TAPS):
            m = mod[t * 16:(t + 1) * 16]
            for k in range(4):
                lo = t * 64 + k * 16
                modulated[lo:lo + 16, :] = (m * sampled[y, lo:lo + 16, :]).astype(BF)
        joined[y + 1, 64:128, 0:COLS] = jnp.dot(
            wd[...], modulated[...], preferred_element_type=F32).astype(BF)
        return 0

    rows_loop(2, ROWS - 2, aligned_row)

    wait_recv(S_CURM, RIGHT, got_cur.at[0])
    wait_recv(S_CURM, LEFT, got_cur.at[1])
    for y in range(ROWS):
        joined[y + 1, 0:64, COLS:WIDE] = unpack(
            got_cur[0].astype(F32), got_cur[1].astype(F32), y).astype(BF)
    row_in(S_H1_IN, h1, 2, 1)
    row_in(S_H1, h1, 2, 0)
    rows_send(S_CUR, joined.at[1, 0:64], joined.at[ROWS + 1, 0:64],
              joined.at[ROWS, 0:64], joined.at[0, 0:64])
    rows_loop(0, 4, ring4(h2_row))
    aligned_row(0, 0)
    aligned_row(ROWS - 1, 0)

    send(S_AL, UP, joined.at[1, 64:128, 0:COLS], joined.at[ROWS + 1, 64:128, 0:COLS])
    send(S_AL, DOWN, joined.at[ROWS, 64:128, 0:COLS], joined.at[0, 64:128, 0:COLS])
    aligned_row(1, 0)
    aligned_row(ROWS - 2, 0)
    def corner_tile(i):
        first = joined[i, 64:128, 0:BLK].astype(F32)
        last = joined[i, 64:128, COLS - BLK:COLS].astype(F32)
        return squeeze(jnp.where(lane < 64, first, last))

    sq_out[S_ALM, 0] = corner_tile(1)
    sq_out[S_ALM, 1] = corner_tile(ROWS)
    for side, d in AL_CORNERS:
        send(S_ALM, d, sq_out.at[S_ALM, side], got_corner.at[OPP[d]])
    pack_al[0] = pack_tiles(
        [joined[y + 1, 64:128, 0:BLK].astype(F32) for y in range(ROWS)], 0).astype(BF)
    pack_al[1] = pack_tiles(
        [joined[y + 1, 64:128, COLS - BLK:COLS].astype(F32) for y in range(ROWS)], 1).astype(BF)
    send(S_ALM, LEFT, pack_al.at[0], got_al.at[0])
    send(S_ALM, RIGHT, pack_al.at[1], got_al.at[1])
    wait_recv(S_ALM, RIGHT, got_al.at[0])
    wait_recv(S_ALM, LEFT, got_al.at[1])
    for y in range(ROWS):
        joined[y + 1, 64:128, COLS:WIDE] = unpack(
            got_al[0].astype(F32), got_al[1].astype(F32), y).astype(BF)

    def corners_in():
        for _, d in AL_CORNERS:
            wait_recv(S_ALM, d, got_corner.at[d])

        def put(i, from_right, from_left):
            for k in range(4):
                a, b = expand(got_corner[from_right], k), expand(got_corner[from_left], k)
                wide = jnp.where(lane < 8, a, jnp.where(lane >= 120, b, 0.0))
                joined[i, 64 + 16 * k:80 + 16 * k, COLS:WIDE] = wide.astype(BF)

        pl.when(has_up)(lambda: put(0, UR, UL))
        pl.when(has_down)(lambda: put(ROWS + 1, DR, DL))

    def t0_row(y, _):
        t0[y + 2] = leaky(conv_row(joined, y, wg[...])).astype(BF)
        return 0

    def inner_row(dst, src, r):
        def go(y, _):
            v = jnp.maximum(conv_row(src, y + 1, wr[r]), 0.0)
            dst[y + 1] = jnp.where(in_frame(y), v, 0.0).astype(BF)
            return 0
        return go

    def t1_row(y, _):
        t1[y + 2] = (t0[y + 2].astype(F32) + conv_row(i0, y, wr[1])).astype(BF)
        return 0

    def out_copy(y):
        return pltpu.make_async_copy(out_ref.at[y], out_hbm.at[y], out_sem.at[y])

    def final_row(y, _):
        trunk = (t1[y + 2].astype(F32) + conv_row(i1, y, wr[3])).astype(BF)
        trunk = trunk[:, 0:COLS].astype(F32)
        out_ref[y] = (trunk + joined[y + 1, 64:128, 0:COLS].astype(F32)).astype(BF)
        out_copy(y).start()
        return 0

    t0_row(1, 0)
    t0_row(ROWS - 2, 0)
    row_out(S_T0_IN, t0, 2, 1)
    rows_loop(2, ROWS - 2, t0_row)
    rows_recv(S_CUR, joined.at[0, 0:64], joined.at[ROWS + 1, 0:64])
    corners_in()
    wait_recv(S_AL, UP, joined.at[0, 64:128, 0:COLS])
    wait_recv(S_AL, DOWN, joined.at[ROWS + 1, 64:128, 0:COLS])
    t0_row(0, 0)
    t0_row(ROWS - 1, 0)
    row_out(S_T0, t0, 2, 0)
    inner0 = inner_row(i0, t0, 0)
    inner1 = inner_row(i1, t1, 2)
    rows_loop(1, ROWS - 1, inner0)
    rows_loop(2, ROWS - 2, t1_row)
    row_in(S_T0_IN, t0, 2, 1)
    row_in(S_T0, t0, 2, 0)
    rows_loop(0, 4, ring4(inner0))
    t1_row(0, 0)
    t1_row(ROWS - 1, 0)
    row_out(S_T1, t1, 2, 0)
    t1_row(1, 0)
    t1_row(ROWS - 2, 0)
    row_out(S_T1_IN, t1, 2, 1)
    rows_loop(1, ROWS - 1, inner1)
    rows_loop(2, ROWS - 2, final_row)
    row_in(S_T1, t1, 2, 0)
    inner1(0, 0)
    inner1(ROWS - 1, 0)
    final_row(1, 0)
    final_row(ROWS - 2, 0)
    row_in(S_T1_IN, t1, 2, 1)
    inner1(-1, 0)
    inner1(ROWS, 0)
    final_row(0, 0)
    final_row(ROWS - 1, 0)

    for y in range(ROWS):
        out_copy(y).wait()
    wait_send(S_OFF, LEFT, pack_off.at[0])
    wait_send(S_OFF, RIGHT, pack_off.at[1])
    by_reach(lat, source_columns_sent)
    source_rows_sent()
    each_relay(relay_sent)
    rows_sent(S_PART, part_out.at[0], part_out.at[1])
    for side, d in AL_CORNERS:
        wait_send(S_ALM, d, sq_out.at[S_ALM, side])
    wait_send(S_ALM, LEFT, pack_al.at[0])
    wait_send(S_ALM, RIGHT, pack_al.at[1])
    wait_send(S_CURM, LEFT, pack_cur.at[0])
    wait_send(S_CURM, RIGHT, pack_cur.at[1])
    rows_sent(S_CUR, joined.at[1, 0:64], joined.at[ROWS, 0:64])
    wait_send(S_AL, UP, joined.at[1, 64:128, 0:COLS])
    wait_send(S_AL, DOWN, joined.at[ROWS, 64:128, 0:COLS])
    for kind, buf in ((S_H1, h1), (S_T0, t0), (S_T1, t1)):
        row_sent(kind, buf, 2, 0)
        row_sent(kind + 1, buf, 2, 1)


def shards(
    offset_input, current, source, first_weight, second_weight, mask_weight, deform_weight,
    merge_weight, residual_weight, footprint, tile_scale, hats,
):
    n_lon, n_lat = lax.axis_size("lon"), lax.axis_size("lat")
    assert n_lon & (n_lon - 1) == 0
    hbm = pl.BlockSpec(memory_space=pl.ANY)
    V = pltpu.VMEM
    out = pl.pallas_call(
        functools.partial(kernel, n_lon, n_lat),
        out_shape=jax.ShapeDtypeStruct((ROWS, 64, COLS), BF),
        in_specs=[hbm] * 12,
        out_specs=hbm,
        scratch_shapes=[
            pltpu.SMEM((ROWS, NB, 2, TAPS), jnp.int32), pltpu.SMEM((ROWS, NB, 2, TAPS), F32),
            V((ROWS, 64, COLS), BF),
            V((9, 64, CIN), BF), V((9, 64, 64), BF), V((9, 64, 144), BF), V((9, 64, 64), BF),
            V((9, 64, 128), BF), V((4, 9, 64, 64), BF),
            V((CIN * ROWS, COLS), BF), V((64 * ROWS, COLS), BF), V((64 * ROWS, COLS), BF),
            V((NB, CIN * ROWS, BLK), F32),
            V((NB, 64 * ROWS, BLK), F32),
            V((ROWS, NB * K2 * BLK, BLK), BF),
            V((ROWS, WIN_COLS, 64, BLK), BF),
            V((WIN_ROWS, WIN_COLS, 64, BLK), BF),
            V((ROWS, TAPS * 64, COLS), F32),
            V((TAPS * 64, COLS), BF),
            V((ROWS + 2, CPAD, WIDE), BF),
            V((ROWS + 4, 64, WIDE), BF),
            V((ROWS + 2, 192, WIDE), BF),
            V((ROWS + 2, 128, WIDE), BF),
            V((ROWS + 4, 64, WIDE), BF),
            V((ROWS + 2, 64, WIDE), BF),
            V((ROWS + 4, 64, WIDE), BF),
            V((ROWS + 2, 64, WIDE), BF),
            V((192, 3 * CPAD), BF), V((192, 192), BF), V((144, 576), BF), V((64, 576), BF),
            V((192, 384), BF), V((4, 192, 192), BF),
            V((2, 208, BLK), BF), V((2, 208, BLK), BF),
            V((2, 64, BLK), BF), V((2, 64, BLK), BF),
            V((2, 64, BLK), BF), V((2, 64, BLK), BF), V((8, 16, BLK), BF),
            V((2, 64, WIDE), BF), V((2, 64, WIDE), BF), V((2, 64, WIDE), F32),
            V((KINDS, 2, 16, BLK), BF), V((KINDS, 2, 16, BLK), BF),
            pltpu.SemaphoreType.DMA((13,)),
            pltpu.SemaphoreType.DMA((ROWS,)),
            pltpu.SemaphoreType.DMA((ROWS,)),
            pltpu.SemaphoreType.DMA((2 * KINDS, 8)),
            pltpu.SemaphoreType.DMA((2 * KINDS, 8)),
        ],
        compiler_params=pltpu.CompilerParams(
            collective_id=0, has_side_effects=True, vmem_limit_bytes=60 * 2**20),
    )(
        offset_input.reshape(CIN * ROWS, COLS),
        current.reshape(64 * ROWS, COLS),
        source.reshape(64 * ROWS, COLS),
        first_weight, second_weight, mask_weight.transpose(0, 2, 1), deform_weight, merge_weight,
        residual_weight.reshape(4, 9, 64, 64),
        footprint.transpose(0, 1, 3, 2), tile_scale.transpose(0, 1, 3, 2),
        hats.reshape(ROWS, NB * K2 * BLK, BLK),
    )
    return out.transpose(1, 0, 2)


def solution(mesh):
    in_specs = (
        P(None, "lat", "lon"),
        P(None, "lat", "lon"),
        P(None, "lat", "lon"),
        P(),
        P(),
        P(),
        P(),
        P(),
        P(),
        P("lat", "lon", None, None),
        P("lat", "lon", None, None),
        P("lat", "lon", None, None, None, None),
    )
    return jax.shard_map(
        shards, mesh=mesh, in_specs=in_specs, out_specs=P(None, "lat", "lon"), check_vma=False)
```

```python
import functools

import jax
import jax.numpy as jnp
from jax import lax
from jax.experimental import pallas as pl
from jax.experimental.pallas import tpu as pltpu
from jax.sharding import PartitionSpec as P

BF = jnp.bfloat16
F32 = jnp.float32
MESH = pl.DeviceIdType.MESH

BLK = 128
ROWS = 8
COLS = 512
WIDE = 640
CIN = 196
CPAD = 256
NB = COLS // BLK
WIN_ROWS = ROWS + 4
WIN_COLS = NB + 4
TAPS = 9
K2 = 18

LEFT, RIGHT, UP, DOWN, UL, UR, DL, DR = range(8)
AL_CORNERS = ((0, UL), (0, UR), (1, DL), (1, DR))
OPP = (RIGHT, LEFT, DOWN, UP, DR, DL, UR, UL)
(S_OFF, S_SRC, S_SRC_LO, S_SRC_HI, S_CURM, S_CUR, S_PART, S_H1, S_H1_IN, S_ALM, S_AL,
 S_T0, S_T0_IN, S_T1, S_T1_IN) = range(15)
KINDS = 15


def leaky(v):
    return jnp.where(v > 0, v, 0.1 * v)


def kernel(
    n_lon, n_lat,
    off_hbm, cur_hbm, src_hbm, w1_hbm, w2_hbm, wm_hbm, wd_hbm, wg_hbm, wr_hbm,
    foot_hbm, scale_hbm, hats_hbm, out_hbm,
    foot_ref, scale_ref, out_ref,
    w1_ref, w2_ref, wm_ref, wd_ref, wg_ref, wr_ref,
    raw_off, raw_src, raw_cur, stage, stage2, hats, near, win, sampled, modulated,
    v0, h1, h2, joined, t0, i0, t1, i1,
    w1, w2, wm, wd, wg, wr,
    pack_off, got_off, pack_cur, got_cur, pack_al, got_al, got_corner,
    part_out, part_in, part_own, sq_out, sq_in,
    load_sem, hat_sem, out_sem, send_sem, recv_sem,
):
    lon = lax.axis_index("lon")
    lat = lax.axis_index("lat")
    left = lax.rem(lon + n_lon - 1, n_lon)
    right = lax.rem(lon + 1, n_lon)
    has_up = lat > 0
    has_down = lat < n_lat - 1
    nb = {
        LEFT: (None, (left, lat)), RIGHT: (None, (right, lat)),
        UP: (has_up, (lon, lat - 1)), DOWN: (has_down, (lon, lat + 1)),
        UL: (has_up, (left, lat - 1)), UR: (has_up, (right, lat - 1)),
        DL: (has_down, (left, lat + 1)), DR: (has_down, (right, lat + 1)),
    }

    def guarded(cond, fn):
        if cond is None:
            fn()
        else:
            pl.when(cond)(fn)

    def copy(kind, direction, src, dst):
        return pltpu.make_async_remote_copy(
            src_ref=src, dst_ref=dst,
            send_sem=send_sem.at[kind, direction],
            recv_sem=recv_sem.at[kind, OPP[direction]],
            device_id=nb[direction][1], device_id_type=MESH,
        )

    def send(kind, direction, src, dst):
        guarded(nb[direction][0], lambda: copy(kind, direction, src, dst).start())

    def wait_send(kind, direction, src):
        def go():
            pltpu.make_async_remote_copy(
                src_ref=src, dst_ref=src, send_sem=send_sem.at[kind, direction],
                recv_sem=recv_sem.at[kind, direction],
                device_id=nb[direction][1], device_id_type=MESH,
            ).wait_send()
        guarded(nb[direction][0], go)

    def wait_recv(kind, direction, dst):
        def go():
            pltpu.make_async_remote_copy(
                src_ref=dst, dst_ref=dst, send_sem=send_sem.at[kind, direction],
                recv_sem=recv_sem.at[kind, direction],
                device_id=nb[direction][1], device_id_type=MESH,
            ).wait_recv()
        guarded(nb[direction][0], go)

    barrier = pltpu.get_barrier_semaphore()
    for d in range(8):
        guarded(nb[d][0], lambda d=d: pl.semaphore_signal(
            barrier, inc=1, device_id=nb[d][1], device_id_type=MESH))

    def off_load(lo, hi, n):
        return pltpu.make_async_copy(off_hbm.at[:, lo:hi], raw_off.at[:, lo:hi], load_sem.at[n])

    load_off = [off_load(0, BLK, 0), off_load(COLS - BLK, COLS, 11), off_load(BLK, COLS - BLK, 12)]
    load_src = pltpu.make_async_copy(src_hbm, raw_src, load_sem.at[1])
    load_cur = pltpu.make_async_copy(cur_hbm, raw_cur, load_sem.at[2])
    for load in load_off:
        load.start()
    load_src.start()
    load_weights = [
        pltpu.make_async_copy(a, b, load_sem.at[3 + n])
        for n, (a, b) in enumerate((
            (w1_hbm, w1_ref), (w2_hbm, w2_ref), (wm_hbm, wm_ref), (wd_hbm, wd_ref),
            (wg_hbm, wg_ref), (wr_hbm, wr_ref), (foot_hbm, foot_ref), (scale_hbm, scale_ref)))
    ]
    for load in load_weights:
        load.start()
    load_cur.start()

    def hat_load(y):
        return pltpu.make_async_copy(hats_hbm.at[y], hats.at[y], hat_sem.at[y])

    def zero_rows(buf, lo, hi):
        buf[lo:hi] = jnp.zeros((hi - lo,) + buf.shape[1:], buf.dtype)

    def no_halo(top):
        for buf, m in ((h1, 2), (joined, 1), (t0, 2), (t1, 2)):
            if top:
                zero_rows(buf, 0, m)
            else:
                zero_rows(buf, ROWS + m, ROWS + 2 * m)
        n = 0 if top else 1
        zero_rows(part_in, n, n + 1)

    pl.when(jnp.logical_not(has_up))(lambda: no_halo(True))
    pl.when(jnp.logical_not(has_down))(lambda: no_halo(False))

    def all_here():
        both = has_up & has_down
        pl.when(both)(lambda: pl.semaphore_wait(barrier, 8))
        pl.when(jnp.logical_not(both))(lambda: pl.semaphore_wait(barrier, 5))

    zero_rows(v0, 0, 1)
    zero_rows(v0, ROWS + 1, ROWS + 2)
    pack_off[...] = jnp.zeros(pack_off.shape, BF)
    for i in range(1, ROWS + 1):
        v0[i, 192:CPAD, :] = jnp.zeros((CPAD - 192, WIDE), BF)

    lane = lax.broadcasted_iota(jnp.int32, (1, BLK), 1)

    def pack_tiles(tiles, side):
        total = None
        for y, tile in enumerate(tiles):
            shift = 8 * y if side == 0 else 8 * y + 8
            moved = pltpu.roll(tile, shift, 1) if shift else tile
            here = (lane >= 8 * y) & (lane < 8 * y + 8)
            total = jnp.where(here, moved, 0.0 if total is None else total)
        return total

    def unpack(from_right, from_left, y):
        a = pltpu.roll(from_right, (128 - 8 * y) % 128, 1) if y else from_right
        b = pltpu.roll(from_left, 120 - 8 * y, 1)
        return jnp.where(lane < 8, a, jnp.where(lane >= 120, b, 0.0))

    def squeeze(tile):
        total = jnp.zeros((16, BLK), F32)
        for k in range(4):
            moved = pltpu.roll(tile[16 * k:16 * k + 16], 16 * k + 8, 1)
            total = jnp.where((lane >= 16 * k) & (lane < 16 * k + 16), moved, total)
        return total.astype(BF)

    def expand(small, k):
        return pltpu.roll(small.astype(F32), 120 - 16 * k, 1)

    def put_margin(row, small, there):
        for k in range(4):
            wide = jnp.where(((lane < 8) | (lane >= 120)) & there, expand(small, k), 0.0)
            row[16 * k:16 * k + 16, COLS:WIDE] = wide.astype(BF)

    def rows_send(kind, up_row, up_dst, down_row, down_dst):
        send(kind, UP, up_row.at[:, 0:COLS], up_dst.at[:, 0:COLS])
        send(kind, DOWN, down_row.at[:, 0:COLS], down_dst.at[:, 0:COLS])
        sq_out[kind, 0] = squeeze(up_row[:, COLS:WIDE].astype(F32))
        sq_out[kind, 1] = squeeze(down_row[:, COLS:WIDE].astype(F32))
        send(kind + KINDS, UP, sq_out.at[kind, 0], sq_in.at[kind, 1])
        send(kind + KINDS, DOWN, sq_out.at[kind, 1], sq_in.at[kind, 0])

    def rows_recv(kind, up_dst, down_dst):
        wait_recv(kind + KINDS, UP, sq_in.at[kind, 0])
        wait_recv(kind + KINDS, DOWN, sq_in.at[kind, 1])
        wait_recv(kind, UP, up_dst.at[:, 0:COLS])
        wait_recv(kind, DOWN, down_dst.at[:, 0:COLS])
        put_margin(up_dst, sq_in[kind, 0], has_up)
        put_margin(down_dst, sq_in[kind, 1], has_down)

    def rows_sent(kind, up_row, down_row):
        wait_send(kind, UP, up_row.at[:, 0:COLS])
        wait_send(kind, DOWN, down_row.at[:, 0:COLS])
        wait_send(kind + KINDS, UP, sq_out.at[kind, 0])
        wait_send(kind + KINDS, DOWN, sq_out.at[kind, 1])

    load_off[0].wait()
    load_off[1].wait()
    def stage_off(j):
        stage[j] = raw_off[:, j * BLK:(j + 1) * BLK].astype(F32)

    stage_off(0)
    stage_off(NB - 1)

    def staged(channels, y, j):
        return stage[j, pl.ds(y, channels, stride=ROWS), :]

    pack_off[0, 0:CIN, :] = pack_tiles(
        [staged(CIN, y, 0) for y in range(ROWS)], 0).astype(BF)
    pack_off[1, 0:CIN, :] = pack_tiles(
        [staged(CIN, y, NB - 1) for y in range(ROWS)], 1).astype(BF)
    all_here()
    send(S_OFF, LEFT, pack_off.at[0], got_off.at[0])
    send(S_OFF, RIGHT, pack_off.at[1], got_off.at[1])

    for y in (2, 3, 4, 5, 0, 1, 6, 7):
        hat_load(y).start()

    load_src.wait()
    for j in range(NB):
        stage2[j] = raw_src[:, j * BLK:(j + 1) * BLK].astype(F32)

    def win_row(y, _):
        for k in range(4):
            for j in range(NB):
                near[y, j + 2, k * 16:(k + 1) * 16, :] = stage2[
                    j, pl.ds(k * ROWS + y, 16, stride=4 * ROWS), :].astype(BF)
        return 0

    lax.fori_loop(0, ROWS, win_row, 0)

    def by_reach(row_tile, fn):
        outer = (row_tile < n_lat // 4) | (row_tile >= n_lat - n_lat // 4)
        pl.when(outer)(lambda: fn(2))
        pl.when(jnp.logical_not(outer))(lambda: fn(1))

    def to_left(rows, n, buf=win):
        return buf.at[rows, 2:2 + n]

    def to_right(rows, n, buf=win):
        return buf.at[rows, 6 - n:6]

    def from_left(rows, n, buf=win):
        return buf.at[rows, 2 - n:2]

    def from_right(rows, n, buf=win):
        return buf.at[rows, 6:6 + n]

    INNER, TOP, BOTTOM = slice(0, 8), slice(0, 2), slice(10, 12)
    FIRST, LAST = slice(0, 2), slice(6, 8)
    odd = lax.rem(lon, 2) == 1
    even = jnp.logical_not(odd)

    def source_columns(n):
        send(S_SRC, LEFT, to_left(INNER, n, near), from_right(INNER, n, near))
        send(S_SRC, RIGHT, to_right(INNER, n, near), from_left(INNER, n, near))

    def source_columns_in(n):
        wait_recv(S_SRC, RIGHT, from_right(INNER, n, near))
        wait_recv(S_SRC, LEFT, from_left(INNER, n, near))

    def source_columns_sent(n):
        wait_send(S_SRC, LEFT, to_left(INNER, n, near))
        wait_send(S_SRC, RIGHT, to_right(INNER, n, near))

    def source_rows():
        send(S_SRC, UP, near.at[FIRST, 2:6], win.at[BOTTOM, 2:6])
        send(S_SRC, DOWN, near.at[LAST, 2:6], win.at[TOP, 2:6])

        @pl.when(even)
        def _():
            by_reach(lat - 1, lambda n: send(S_SRC, UL, to_left(FIRST, n, near), from_right(BOTTOM, n)))
            by_reach(lat + 1, lambda n: send(S_SRC, DL, to_left(LAST, n, near), from_right(TOP, n)))

        @pl.when(odd)
        def _():
            by_reach(lat - 1, lambda n: send(S_SRC, UR, to_right(FIRST, n, near), from_left(BOTTOM, n)))
            by_reach(lat + 1, lambda n: send(S_SRC, DR, to_right(LAST, n, near), from_left(TOP, n)))

    def source_rows_sent():
        wait_send(S_SRC, UP, near.at[FIRST, 2:6])
        wait_send(S_SRC, DOWN, near.at[LAST, 2:6])

        @pl.when(even)
        def _():
            by_reach(lat - 1, lambda n: wait_send(S_SRC, UL, to_left(FIRST, n, near)))
            by_reach(lat + 1, lambda n: wait_send(S_SRC, DL, to_left(LAST, n, near)))

        @pl.when(odd)
        def _():
            by_reach(lat - 1, lambda n: wait_send(S_SRC, UR, to_right(FIRST, n, near)))
            by_reach(lat + 1, lambda n: wait_send(S_SRC, DR, to_right(LAST, n, near)))

    def relay(kind, rows, n):
        pl.when(even)(lambda: send(kind, RIGHT, to_right(rows, n), from_left(rows, n)))
        pl.when(odd)(lambda: send(kind, LEFT, to_left(rows, n), from_right(rows, n)))

    def relay_in(kind, rows, n):
        pl.when(even)(lambda: wait_recv(kind, RIGHT, from_right(rows, n)))
        pl.when(odd)(lambda: wait_recv(kind, LEFT, from_left(rows, n)))

    def relay_sent(kind, rows, n):
        pl.when(even)(lambda: wait_send(kind, RIGHT, to_right(rows, n)))
        pl.when(odd)(lambda: wait_send(kind, LEFT, to_left(rows, n)))

    def each_relay(fn):
        pl.when(has_up)(lambda: by_reach(lat, lambda n: fn(S_SRC_LO, TOP, n)))
        pl.when(has_down)(lambda: by_reach(lat, lambda n: fn(S_SRC_HI, BOTTOM, n)))

    def source_rows_in():
        wait_recv(S_SRC, UP, win.at[TOP, 2:6])
        wait_recv(S_SRC, DOWN, win.at[BOTTOM, 2:6])
        each_relay(relay)

    def source_corners_in():
        @pl.when(odd)
        def _():
            by_reach(lat, lambda n: wait_recv(S_SRC, UR, from_right(TOP, n)))
            by_reach(lat, lambda n: wait_recv(S_SRC, DR, from_right(BOTTOM, n)))

        @pl.when(even)
        def _():
            by_reach(lat, lambda n: wait_recv(S_SRC, UL, from_left(TOP, n)))
            by_reach(lat, lambda n: wait_recv(S_SRC, DL, from_left(BOTTOM, n)))

        each_relay(relay_in)

    by_reach(lat, source_columns)
    source_rows()

    load_off[2].wait()
    for j in range(1, NB - 1):
        stage_off(j)

    def v0_row(y, _):
        for j in range(NB):
            v0[y + 1, 0:CIN, j * BLK:(j + 1) * BLK] = staged(CIN, y, j).astype(BF)
        return 0

    lax.fori_loop(0, ROWS, v0_row, 0)

    load_cur.wait()
    for j in range(NB):
        stage2[j] = raw_cur[:, j * BLK:(j + 1) * BLK].astype(F32)

    def cur_staged(y, j):
        return stage2[j, pl.ds(y, 64, stride=ROWS), :]

    def cur_row(y, _):
        for j in range(NB):
            joined[y + 1, 0:64, j * BLK:(j + 1) * BLK] = cur_staged(y, j).astype(BF)
        return 0

    lax.fori_loop(0, ROWS, cur_row, 0)
    pack_cur[0] = pack_tiles([cur_staged(y, 0) for y in range(ROWS)], 0).astype(BF)
    pack_cur[1] = pack_tiles([cur_staged(y, NB - 1) for y in range(ROWS)], 1).astype(BF)

    send(S_CURM, LEFT, pack_cur.at[0], got_cur.at[0])
    send(S_CURM, RIGHT, pack_cur.at[1], got_cur.at[1])

    for load in load_weights:
        load.wait()
    w1[...] = jnp.zeros(w1.shape, BF)
    for a in range(3):
        for b in range(3):
            w1[b * 64:(b + 1) * 64, a * CPAD:a * CPAD + CIN] = w1_ref[3 * a + b]
            wg[b * 64:(b + 1) * 64, a * 128:(a + 1) * 128] = wg_ref[3 * a + b]
    for b in range(3):
        w2[b * 64:(b + 1) * 64, :] = jnp.concatenate([w2_ref[3 * a + b] for a in range(3)], axis=1)
        for r in range(4):
            wr[r, b * 64:(b + 1) * 64, :] = jnp.concatenate(
                [wr_ref[r, 3 * a + b] for a in range(3)], axis=1)
    wm[...] = wm_ref[...].reshape(TAPS * 64, 144).astype(F32).T.astype(BF)
    row_id = lax.broadcasted_iota(jnp.int32, (64, 64), 0)
    col_id = lax.broadcasted_iota(jnp.int32, (64, 64), 1)
    perm = (row_id == (col_id % 16) * 4 + col_id // 16).astype(BF)
    wd[...] = jnp.concatenate(
        [jnp.dot(wd_ref[t], perm, preferred_element_type=F32).astype(BF) for t in range(TAPS)], axis=1)

    def spread(p):
        n = p.shape[1]
        return pltpu.roll(p[0:64], 1, 1) + p[64:128] + pltpu.roll(p[128:192], n - 1, 1)

    def conv_row(src, i, weight):
        x = src[pl.ds(i, 3)].reshape(3 * src.shape[1], WIDE)
        return spread(jnp.dot(weight, x, preferred_element_type=F32))

    def row_out(kind, buf, m, n):
        rows_send(kind, buf.at[m + n], buf.at[ROWS + m + n],
                  buf.at[ROWS + m - 1 - n], buf.at[m - 1 - n])

    def row_in(kind, buf, m, n):
        rows_recv(kind, buf.at[m - 1 - n], buf.at[ROWS + m + n])

    def row_sent(kind, buf, m, n):
        rows_sent(kind, buf.at[m + n], buf.at[ROWS + m - 1 - n])

    def rows_loop(lo, hi, fn):
        lax.fori_loop(lo, hi, fn, 0, unroll=True)

    def edge4(fn):
        return lambda i, c: fn(i + (i // 2) * (ROWS - 4), c)

    def ring4(fn):
        return lambda i, c: fn(i - 1 + (i // 2) * (ROWS - 2), c)

    wait_recv(S_OFF, RIGHT, got_off.at[0])
    wait_recv(S_OFF, LEFT, got_off.at[1])
    def v0_margin(y):
        v0[y + 1, 0:CIN, COLS:WIDE] = unpack(
            got_off[0, 0:CIN, :].astype(F32), got_off[1, 0:CIN, :].astype(F32), y).astype(BF)

    v0_margin(0)
    v0_margin(ROWS - 1)
    part_out[0] = spread(jnp.dot(w1[:, 2 * CPAD:], v0[1], preferred_element_type=F32)).astype(BF)
    part_out[1] = spread(jnp.dot(w1[:, :CPAD], v0[ROWS], preferred_element_type=F32)).astype(BF)
    rows_send(S_PART, part_out.at[0], part_in.at[1], part_out.at[1], part_in.at[0])
    for y in range(1, ROWS - 1):
        v0_margin(y)

    def h1_row(y, _):
        h1[y + 2] = leaky(conv_row(v0, y, w1[...])).astype(BF)
        return 0

    h1_row(1, 0)
    h1_row(ROWS - 2, 0)
    row_out(S_H1_IN, h1, 2, 1)
    rows_loop(2, ROWS - 2, h1_row)
    part_own[0] = conv_row(v0, 0, w1[...])
    part_own[1] = conv_row(v0, ROWS - 1, w1[...])

    total = NB * n_lon
    shift = total.bit_length() - 1
    col_base = lon * NB - 2

    def sample_row(y, src, first, count):
        for j in range(NB):
            for t in range(TAPS):
                parts = []
                for f in range(2):
                    ix = foot_ref[y, j, f, t]
                    row = jnp.clip(lax.shift_right_logical(ix, shift) - first, 0, count - 1)
                    col = jnp.minimum(lax.bitwise_and(ix - col_base, total - 1), WIN_COLS - 1)
                    parts.append((src[row, col].astype(F32) * scale_ref[y, j, f, t]).astype(BF))
                tile = hats[y, (j * K2 + 2 * t) * BLK:(j * K2 + 2 * t + 2) * BLK, :]
                sampled[y, t * 64:(t + 1) * 64, j * BLK:(j + 1) * BLK] = jnp.dot(
                    jnp.concatenate(parts, axis=1), tile, preferred_element_type=F32)
        return 0

    by_reach(lat, source_columns_in)
    for y in range(2, ROWS - 2):
        hat_load(y).wait()
    rows_loop(2, ROWS - 2, lambda y, _: sample_row(y, near, lat * ROWS, ROWS))
    win[2:2 + ROWS] = near[...]
    source_rows_in()

    rows_recv(S_PART, part_in.at[0], part_in.at[1])
    h1[2] = leaky(part_own[0] + part_in[0].astype(F32)).astype(BF)
    h1[ROWS + 1] = leaky(part_own[1] + part_in[1].astype(F32)).astype(BF)

    row_out(S_H1, h1, 2, 0)

    def in_frame(y):
        g = lat * ROWS + y
        return (g >= 0) & (g < n_lat * ROWS)

    def h2_row(y, _):
        v = leaky(conv_row(h1, y + 1, w2[...]))
        v = jnp.where(in_frame(y), v, 0.0)
        h2[y + 1, 0:64] = pltpu.roll(v, 1, 1).astype(BF)
        h2[y + 1, 64:128] = v.astype(BF)
        h2[y + 1, 128:192] = pltpu.roll(v, WIDE - 1, 1).astype(BF)
        return 0

    rows_loop(1, ROWS - 1, h2_row)

    source_corners_in()
    for y in (0, 1, ROWS - 2, ROWS - 1):
        hat_load(y).wait()
    rows_loop(0, 4, edge4(lambda y, _: sample_row(y, win, lat * ROWS - 2, WIN_ROWS)))

    def aligned_row(y, _):
        half = y % 2
        x = h2[pl.ds(y, 3)].reshape(576, WIDE)[:, 0:COLS]
        logits = jnp.dot(wm[...], x, preferred_element_type=F32)
        mod = 1.0 / (1.0 + jnp.exp(-logits))
        for t in range(TAPS):
            m = mod[t * 16:(t + 1) * 16]
            for k in range(4):
                lo = t * 64 + k * 16
                modulated[half, lo:lo + 16, :] = (m * sampled[y, lo:lo + 16, :]).astype(BF)
        joined[y + 1, 64:128, 0:COLS] = jnp.dot(
            wd[...], modulated[half], preferred_element_type=F32).astype(BF)
        return 0

    rows_loop(2, ROWS - 2, aligned_row)

    wait_recv(S_CURM, RIGHT, got_cur.at[0])
    wait_recv(S_CURM, LEFT, got_cur.at[1])

    def cur_margin(y):
        joined[y + 1, 0:64, COLS:WIDE] = unpack(
            got_cur[0].astype(F32), got_cur[1].astype(F32), y).astype(BF)

    cur_margin(0)
    cur_margin(ROWS - 1)
    rows_send(S_CUR, joined.at[1, 0:64], joined.at[ROWS + 1, 0:64],
              joined.at[ROWS, 0:64], joined.at[0, 0:64])
    row_in(S_H1_IN, h1, 2, 1)
    row_in(S_H1, h1, 2, 0)
    rows_loop(0, 4, ring4(h2_row))
    aligned_row(0, 0)
    aligned_row(ROWS - 1, 0)

    send(S_AL, UP, joined.at[1, 64:128, 0:COLS], joined.at[ROWS + 1, 64:128, 0:COLS])
    send(S_AL, DOWN, joined.at[ROWS, 64:128, 0:COLS], joined.at[0, 64:128, 0:COLS])
    aligned_row(1, 0)
    aligned_row(ROWS - 2, 0)
    def corner_tile(i):
        first = joined[i, 64:128, 0:BLK].astype(F32)
        last = joined[i, 64:128, COLS - BLK:COLS].astype(F32)
        return squeeze(jnp.where(lane < 64, first, last))

    sq_out[S_ALM, 0] = corner_tile(1)
    sq_out[S_ALM, 1] = corner_tile(ROWS)
    for side, d in AL_CORNERS:
        send(S_ALM, d, sq_out.at[S_ALM, side], got_corner.at[OPP[d]])
    pack_al[0] = pack_tiles(
        [joined[y + 1, 64:128, 0:BLK].astype(F32) for y in range(ROWS)], 0).astype(BF)
    pack_al[1] = pack_tiles(
        [joined[y + 1, 64:128, COLS - BLK:COLS].astype(F32) for y in range(ROWS)], 1).astype(BF)
    send(S_ALM, LEFT, pack_al.at[0], got_al.at[0])
    send(S_ALM, RIGHT, pack_al.at[1], got_al.at[1])
    for y in range(1, ROWS - 1):
        cur_margin(y)
    wait_recv(S_ALM, RIGHT, got_al.at[0])
    wait_recv(S_ALM, LEFT, got_al.at[1])
    for y in range(ROWS):
        joined[y + 1, 64:128, COLS:WIDE] = unpack(
            got_al[0].astype(F32), got_al[1].astype(F32), y).astype(BF)

    def corners_in():
        for _, d in AL_CORNERS:
            wait_recv(S_ALM, d, got_corner.at[d])

        def put(i, from_right, from_left):
            for k in range(4):
                a, b = expand(got_corner[from_right], k), expand(got_corner[from_left], k)
                wide = jnp.where(lane < 8, a, jnp.where(lane >= 120, b, 0.0))
                joined[i, 64 + 16 * k:80 + 16 * k, COLS:WIDE] = wide.astype(BF)

        pl.when(has_up)(lambda: put(0, UR, UL))
        pl.when(has_down)(lambda: put(ROWS + 1, DR, DL))

    def t0_row(y, _):
        t0[y + 2] = leaky(conv_row(joined, y, wg[...])).astype(BF)
        return 0

    def inner_row(dst, src, r):
        def go(y, _):
            v = jnp.maximum(conv_row(src, y + 1, wr[r]), 0.0)
            dst[y + 1] = jnp.where(in_frame(y), v, 0.0).astype(BF)
            return 0
        return go

    def t1_row(y, _):
        t1[y + 2] = (t0[y + 2].astype(F32) + conv_row(i0, y, wr[1])).astype(BF)
        return 0

    def out_copy(y):
        return pltpu.make_async_copy(out_ref.at[y], out_hbm.at[y], out_sem.at[y])

    def final_row(y, _):
        trunk = (t1[y + 2].astype(F32) + conv_row(i1, y, wr[3])).astype(BF)
        trunk = trunk[:, 0:COLS].astype(F32)
        out_ref[y] = (trunk + joined[y + 1, 64:128, 0:COLS].astype(F32)).astype(BF)
        out_copy(y).start()
        return 0

    t0_row(1, 0)
    t0_row(ROWS - 2, 0)
    row_out(S_T0_IN, t0, 2, 1)
    rows_loop(2, ROWS - 2, t0_row)
    rows_recv(S_CUR, joined.at[0, 0:64], joined.at[ROWS + 1, 0:64])
    corners_in()
    wait_recv(S_AL, UP, joined.at[0, 64:128, 0:COLS])
    wait_recv(S_AL, DOWN, joined.at[ROWS + 1, 64:128, 0:COLS])
    t0_row(0, 0)
    t0_row(ROWS - 1, 0)
    row_out(S_T0, t0, 2, 0)
    inner0 = inner_row(i0, t0, 0)
    inner1 = inner_row(i1, t1, 2)
    rows_loop(1, ROWS - 1, inner0)
    rows_loop(2, ROWS - 2, t1_row)
    row_in(S_T0_IN, t0, 2, 1)
    row_in(S_T0, t0, 2, 0)
    rows_loop(0, 4, ring4(inner0))
    t1_row(0, 0)
    t1_row(ROWS - 1, 0)
    row_out(S_T1, t1, 2, 0)
    t1_row(1, 0)
    t1_row(ROWS - 2, 0)
    row_out(S_T1_IN, t1, 2, 1)
    rows_loop(1, ROWS - 1, inner1)
    rows_loop(2, ROWS - 2, final_row)
    row_in(S_T1, t1, 2, 0)
    inner1(0, 0)
    inner1(ROWS - 1, 0)
    final_row(1, 0)
    final_row(ROWS - 2, 0)
    row_in(S_T1_IN, t1, 2, 1)
    inner1(-1, 0)
    inner1(ROWS, 0)
    final_row(0, 0)
    final_row(ROWS - 1, 0)

    for y in range(ROWS):
        out_copy(y).wait()
    wait_send(S_OFF, LEFT, pack_off.at[0])
    wait_send(S_OFF, RIGHT, pack_off.at[1])
    by_reach(lat, source_columns_sent)
    source_rows_sent()
    each_relay(relay_sent)
    rows_sent(S_PART, part_out.at[0], part_out.at[1])
    for side, d in AL_CORNERS:
        wait_send(S_ALM, d, sq_out.at[S_ALM, side])
    wait_send(S_ALM, LEFT, pack_al.at[0])
    wait_send(S_ALM, RIGHT, pack_al.at[1])
    wait_send(S_CURM, LEFT, pack_cur.at[0])
    wait_send(S_CURM, RIGHT, pack_cur.at[1])
    rows_sent(S_CUR, joined.at[1, 0:64], joined.at[ROWS, 0:64])
    wait_send(S_AL, UP, joined.at[1, 64:128, 0:COLS])
    wait_send(S_AL, DOWN, joined.at[ROWS, 64:128, 0:COLS])
    for kind, buf in ((S_H1, h1), (S_T0, t0), (S_T1, t1)):
        row_sent(kind, buf, 2, 0)
        row_sent(kind + 1, buf, 2, 1)


def shards(
    offset_input, current, source, first_weight, second_weight, mask_weight, deform_weight,
    merge_weight, residual_weight, footprint, tile_scale, hats,
):
    n_lon, n_lat = lax.axis_size("lon"), lax.axis_size("lat")
    assert n_lon & (n_lon - 1) == 0
    hbm = pl.BlockSpec(memory_space=pl.ANY)
    V = pltpu.VMEM
    out = pl.pallas_call(
        functools.partial(kernel, n_lon, n_lat),
        out_shape=jax.ShapeDtypeStruct((ROWS, 64, COLS), BF),
        in_specs=[hbm] * 12,
        out_specs=hbm,
        scratch_shapes=[
            pltpu.SMEM((ROWS, NB, 2, TAPS), jnp.int32), pltpu.SMEM((ROWS, NB, 2, TAPS), F32),
            V((ROWS, 64, COLS), BF),
            V((9, 64, CIN), BF), V((9, 64, 64), BF), V((9, 64, 144), BF), V((9, 64, 64), BF),
            V((9, 64, 128), BF), V((4, 9, 64, 64), BF),
            V((CIN * ROWS, COLS), BF), V((64 * ROWS, COLS), BF), V((64 * ROWS, COLS), BF),
            V((NB, CIN * ROWS, BLK), F32),
            V((NB, 64 * ROWS, BLK), F32),
            V((ROWS, NB * K2 * BLK, BLK), BF),
            V((ROWS, WIN_COLS, 64, BLK), BF),
            V((WIN_ROWS, WIN_COLS, 64, BLK), BF),
            V((ROWS, TAPS * 64, COLS), F32),
            V((2, TAPS * 64, COLS), BF),
            V((ROWS + 2, CPAD, WIDE), BF),
            V((ROWS + 4, 64, WIDE), BF),
            V((ROWS + 2, 192, WIDE), BF),
            V((ROWS + 2, 128, WIDE), BF),
            V((ROWS + 4, 64, WIDE), BF),
            V((ROWS + 2, 64, WIDE), BF),
            V((ROWS + 4, 64, WIDE), BF),
            V((ROWS + 2, 64, WIDE), BF),
            V((192, 3 * CPAD), BF), V((192, 192), BF), V((144, 576), BF), V((64, 576), BF),
            V((192, 384), BF), V((4, 192, 192), BF),
            V((2, 208, BLK), BF), V((2, 208, BLK), BF),
            V((2, 64, BLK), BF), V((2, 64, BLK), BF),
            V((2, 64, BLK), BF), V((2, 64, BLK), BF), V((8, 16, BLK), BF),
            V((2, 64, WIDE), BF), V((2, 64, WIDE), BF), V((2, 64, WIDE), F32),
            V((KINDS, 2, 16, BLK), BF), V((KINDS, 2, 16, BLK), BF),
            pltpu.SemaphoreType.DMA((13,)),
            pltpu.SemaphoreType.DMA((ROWS,)),
            pltpu.SemaphoreType.DMA((ROWS,)),
            pltpu.SemaphoreType.DMA((2 * KINDS, 8)),
            pltpu.SemaphoreType.DMA((2 * KINDS, 8)),
        ],
        compiler_params=pltpu.CompilerParams(
            collective_id=0, has_side_effects=True, vmem_limit_bytes=60 * 2**20),
    )(
        offset_input.reshape(CIN * ROWS, COLS),
        current.reshape(64 * ROWS, COLS),
        source.reshape(64 * ROWS, COLS),
        first_weight, second_weight, mask_weight.transpose(0, 2, 1), deform_weight, merge_weight,
        residual_weight.reshape(4, 9, 64, 64),
        footprint.transpose(0, 1, 3, 2), tile_scale.transpose(0, 1, 3, 2),
        hats.reshape(ROWS, NB * K2 * BLK, BLK),
    )
    return out.transpose(1, 0, 2)


def solution(mesh):
    in_specs = (
        P(None, "lat", "lon"),
        P(None, "lat", "lon"),
        P(None, "lat", "lon"),
        P(),
        P(),
        P(),
        P(),
        P(),
        P(),
        P("lat", "lon", None, None),
        P("lat", "lon", None, None),
        P("lat", "lon", None, None, None, None),
    )
    return jax.shard_map(
        shards, mesh=mesh, in_specs=in_specs, out_specs=P(None, "lat", "lon"), check_vma=False)
```
